32 devices in a mesh: rep: 4 (over z), fsdp: 4 (over y, core), expert: 2 (over x).
Axes of the slice: x: 2, y: 2, z: 4, core: 2. Of those that a mesh axis runs over, the one named last changes fastest.
Arguments:
- tokens: bfloat16 [32768, 768], P(('rep', 'fsdp', 'expert')), may hold values from -6 to 6
- segment_ids: int32 [32, 1024], P(('rep', 'fsdp', 'expert')), may hold values from 0 to 3, never falling along the last dimension, each value on 1 to 512 neighbouring positions
- offset_bucket: int32 [2047], replicated, may hold values from 0 to 31
- routes: int32 [32768, 1], P(('rep', 'fsdp', 'expert')), may hold values from 0 to 1; in each aligned block of 1024 rows (0 to 1023, 1024 to 2047, ...) at most 640 rows name the same one
- capacity_keep: int32 [32768], P(('rep', 'fsdp', 'expert')), may hold values 0 or 1
- gain_attn: bfloat16 [768], P(('fsdp', 'expert')), may hold values from 0.5 to 1.5
- gain_ffn: bfloat16 [768], P(('fsdp', 'expert')), may hold values from 0.5 to 1.5
- w_query: bfloat16 [768, 768], P(('fsdp', 'expert')), may hold values from -0.21875 to 0.21875
- w_key: bfloat16 [768, 768], P(('fsdp', 'expert')), may hold values from -0.21875 to 0.21875
- w_value: bfloat16 [768, 768], P(('fsdp', 'expert')), may hold values from -0.21875 to 0.21875
- w_output: bfloat16 [768, 768], P(('fsdp', 'expert')), may hold values from -0.875 to 0.875
- rel_table: bfloat16 [32, 12], P(('fsdp', 'expert')), may hold values from -4 to 4
- router: bfloat16 [768, 2], P(('fsdp', 'expert')), may hold values from -0.21875 to 0.21875
- expert_in: bfloat16 [2, 768, 3072], P('expert'), may hold values from -0.21875 to 0.21875
- expert_out: bfloat16 [2, 3072, 768], P('expert'), may hold values from -0.21875 to 0.21875
- grad_out: bfloat16 [32768, 768], P(('rep', 'fsdp', 'expert')), may hold values from -6 to 6
Outputs:
- block_output: bfloat16 [32768, 768], P(('rep', 'fsdp', 'expert'))
- grad_tokens: bfloat16 [32768, 768], P(('rep', 'fsdp', 'expert'))
- grad_gain_attn: float32 [768], P(('fsdp', 'expert'))
- grad_gain_ffn: float32 [768], P(('fsdp', 'expert'))
- grad_w_query: float32 [768, 768], P(('fsdp', 'expert'))
- grad_w_key: float32 [768, 768], P(('fsdp', 'expert'))
- grad_w_value: float32 [768, 768], P(('fsdp', 'expert'))
- grad_w_output: float32 [768, 768], P(('fsdp', 'expert'))
- grad_rel_table: float32 [32, 12], P(('fsdp', 'expert'))
- grad_router: float32 [768, 2], P(('fsdp', 'expert'))
- grad_expert_in: float32 [2, 768, 3072], P('expert')
- grad_expert_out: float32 [2, 3072, 768], P('expert')
The draws below stay inside these ranges and needn't reach their ends.
Inputs may be any that keep to these rules, and one draw needn't show every extreme that they name: `routes`: in the rows of one device no expert is named more than 640 times. `segment_ids`: numbers never fall along a sequence; a document has at most 512 positions.
All inputs are finite; a program needn't handle non-finite values. No bound on the sum of `capacity_keep` on one device may be relied on, other than what follows from the above.
Results may differ from the reference program's by a relative error of at most 0.015.
Values may be sent and summed in bfloat16 or wider, within the bound.
No kernel may reach another device: no remote copies, remote signals or barrier semaphores. Data moves between devices by JAX's collectives and lax.ppermute only.
A program may use at most 896 MiB of HBM per device.

```python
import math
import jax
import jax.numpy as jnp
import numpy as np
from jax import lax

D = 768
HEADS = 12
HEAD_DIM = 64
FF = 3072
NB = 32
LEN = 1024
EXPERTS = 2
TOK_DEV = 1024
SEQS = 32
TOKENS = 32768
CAP = 640
DEVICES = 32


def plant(values, rng, smallest, top_value):
    spot = [jax.random.randint(jax.random.fold_in(rng, axis), (), 0, length) for axis, length in enumerate(values.shape)]
    longest = values.shape.index(max(values.shape))
    beside = spot[:longest] + [(spot[longest] + 1) % values.shape[longest]] + spot[longest + 1:]
    return values.at[tuple(spot)].set(smallest).at[tuple(beside)].set(top_value)


def level_of(rng, extent, cuts, least, top_value):
    level, own = 1.0, jax.random.fold_in(rng, 6)
    for axis_at, parts in cuts:
        draws = jnp.exp(jax.random.uniform(jax.random.fold_in(own, axis_at), (parts,), jnp.float32, least / len(cuts), top_value / len(cuts)))
        level = level * jnp.repeat(draws, extent[axis_at] // parts).reshape([-1 if axis == axis_at else 1 for axis in range(len(extent))])
    return level


def split_up(number_of, total, reach, slope):
    weights = [(1 << 20) // math.isqrt(grade ** slope) + 1 for grade in range(2, number_of + 1)]
    surplus, counts = total - reach - (number_of - 1), [1] * (number_of - 1)
    while surplus > 0:
        movable = [i for i in range(number_of - 1) if counts[i] < reach]
        pool, left = sum([weights[i] for i in movable]), surplus
        for i in movable:
            addition = min(reach - counts[i], max(1, left * weights[i] // pool), surplus)
            counts[i] = counts[i] + addition
            surplus = surplus - addition
    return np.array([reach] + counts)


def uneven(own_key, count, total, reach, slope):
    if count == 2:
        one = jax.random.randint(own_key, (), max(1, total - reach), min(reach, total - 1) + 1)
        return jnp.stack([one, total - one])
    tallies = jnp.asarray(split_up(count, total, reach, slope), jnp.int32)
    pairs = (count - 1) // 2
    source_of, taker = tallies[1:1 + 2 * pairs:2], tallies[2:2 + 2 * pairs:2]
    room = jnp.minimum(source_of - 1, reach - taker)
    moved = jax.random.randint(jax.random.fold_in(own_key, 1), (pairs,), 0, 1 << 20) % (room + 1)
    tallies = tallies.at[1:1 + 2 * pairs:2].set(source_of - moved).at[2:2 + 2 * pairs:2].set(taker + moved)
    return tallies[jax.random.permutation(jax.random.fold_in(own_key, 2), count)]


def routed_block(stream_key, own, number, rows, count, top, limit, slope):
    order = jax.random.permutation(stream_key, count)
    crowded, ordinary = shares(count, rows * top, limit, slope, True), shares(count, rows * top, limit, slope, False)
    places = jnp.arange(count)

    def named(tallies, turn):
        used = int((tallies > 0).sum())
        fixed = max(1, used // 4)
        moved = fixed + (places - fixed + turn * (used - fixed)) % max(1, count - fixed)
        return jnp.zeros((count,), jnp.int32).at[order[jnp.where(places < fixed, places, moved)]].set(jnp.asarray(tallies, jnp.int32))

    tallies = jnp.where(number % 4 == 0, named(crowded, number // 4), named(ordinary, number - number // 4 - 1))
    mixed = jax.random.permutation(jax.random.fold_in(own, 3), count)
    giver, taker = mixed[0:count // 2 * 2:2], mixed[1:count // 2 * 2:2]
    margin = jnp.minimum(tallies[giver] - 1, limit - tallies[taker]) // 2
    margin = jnp.where((giver == order[0]) | (taker == order[0]) | (tallies[taker] == 0), 0, jnp.maximum(margin, 0))
    moved = jax.random.randint(jax.random.fold_in(own, 4), (count // 2,), 0, 1 << 20) % (margin + 1)
    tallies = tallies.at[giver].add(-moved).at[taker].add(moved)
    items = jnp.searchsorted(jnp.cumsum(tallies), jnp.arange(rows * top), side="right").astype(jnp.int32)
    grid = items.reshape(top, rows).T
    grid = grid[jax.random.permutation(jax.random.fold_in(own, 1), rows)]
    turn = jax.random.randint(jax.random.fold_in(own, 2), (rows, 1), 0, top)
    return jnp.take_along_axis(grid, (jnp.arange(top)[None, :] + turn) % top, axis=1)


def shares(number_of, total, most, skew, full):
    portions = [(1 << 20) // math.isqrt(rank ** skew) + 1 for rank in range(1, number_of + 1)]
    largest = most if full else min(most, max(-(-total // number_of), total * portions[0] // sum(portions)))
    least = 1 if total - largest >= number_of - 1 else 0
    counts, rest = [largest] + [least] * (number_of - 1), total - largest - least * (number_of - 1)
    while rest > 0:
        movable = [i for i in range(1, number_of) if counts[i] < largest] or [i for i in range(1, number_of) if counts[i] < most]
        mass, budget = sum([portions[i] for i in movable]), rest
        for i in movable:
            more = min(most - counts[i], max(1, budget * portions[i] // mass), rest)
            counts[i] = counts[i] + more
            rest = rest - more
    return np.array(counts)


def noise(own_key, dims, width, bound, split=(), kind=jnp.bfloat16):
    level = level_of(own_key, dims, split, -0.22, 0.18) if split else 1.0
    values = jax.random.normal(own_key, dims, jnp.float32) * width * level
    return jnp.minimum(jnp.maximum(values, -bound), bound).astype(kind)


def setup_inputs(seed: int = 0) -> dict:
    arg_keys = jax.random.split(jax.random.key(seed), 17)
    tokens = noise(arg_keys[0], (TOKENS, D), 1.0, 6.0, ((0, 32),))
    segment_ids = jax.vmap(lambda own: jnp.searchsorted(jnp.cumsum(uneven(own, 4, LEN, LEN // 2, 0)), jnp.arange(LEN), side="right"))(jax.random.split(arg_keys[1], SEQS)).reshape((SEQS, LEN)).astype(jnp.int32)
    offset_bucket = plant(jax.random.randint(arg_keys[2], (2 * LEN - 1,), 0, NB), jax.random.fold_in(arg_keys[2], 1), 0, NB - 1).astype(jnp.int32)
    routes_keys = jax.random.split(jax.random.fold_in(arg_keys[3], 1), TOKENS // TOK_DEV)
    routes_turns = jax.random.permutation(jax.random.fold_in(arg_keys[3], 3), TOKENS // TOK_DEV)
    routes = jax.vmap(lambda own, number: routed_block(jax.random.fold_in(arg_keys[3], 2), own, number, TOK_DEV, EXPERTS, 1, CAP, 2))(routes_keys, routes_turns).reshape((TOKENS, 1))
    capacity_keep = plant((jax.random.randint(arg_keys[4], (TOKENS,), 0, 8) < 7).astype(jnp.int32), jax.random.fold_in(arg_keys[4], 1), 0, 1)
    gain_attn = jnp.clip(1.0 + 0.1 * jax.random.normal(arg_keys[5], (D,), jnp.float32), 0.5, 1.5).astype(jnp.bfloat16)
    gain_ffn = jnp.clip(1.0 + 0.1 * jax.random.normal(arg_keys[6], (D,), jnp.float32), 0.5, 1.5).astype(jnp.bfloat16)
    w_query = noise(arg_keys[7], (D, HEADS * HEAD_DIM), D ** -0.5, 0.21875, ((0, 8),))
    w_key = noise(arg_keys[8], (D, HEADS * HEAD_DIM), D ** -0.5, 0.21875, ((0, 8),))
    w_value = noise(arg_keys[9], (D, HEADS * HEAD_DIM), D ** -0.5, 0.21875, ((0, 8),))
    w_output = noise(arg_keys[10], (HEADS * HEAD_DIM, D), (HEADS * HEAD_DIM // 16) ** -0.5, 0.875, ((0, 8),))
    rel_table = noise(arg_keys[11], (NB, HEADS), 1.0, 4.0, ((0, 8),))
    router = noise(arg_keys[12], (D, EXPERTS), D ** -0.5, 0.21875, ((0, 8),))
    expert_in = noise(arg_keys[13], (EXPERTS, D, FF), D ** -0.5, 0.21875, ((0, 2),))
    expert_out = noise(arg_keys[14], (EXPERTS, FF, D), (max(FF // (EXPERTS * EXPERTS), 1)) ** -0.5, 0.21875, ((0, 2),))
    grad_out = noise(arg_keys[15], (TOKENS, D), 1.0, 6.0, ((0, 32),))
    return dict(tokens=tokens, segment_ids=segment_ids, offset_bucket=offset_bucket, routes=routes, capacity_keep=capacity_keep, gain_attn=gain_attn, gain_ffn=gain_ffn, w_query=w_query, w_key=w_key, w_value=w_value, w_output=w_output, rel_table=rel_table, router=router, expert_in=expert_in, expert_out=expert_out, grad_out=grad_out)


@jax.custom_vjp
def low(v):
    return lax.optimization_barrier(v.astype(jnp.bfloat16)).astype(jnp.float32)

@jax.custom_vjp
def low_back(v):
    return v

def low_keep(v):
    return (low(v), None)

def low_pass(kept, grad):
    return (grad,)

def back_keep(v):
    return (v, None)

def back_low(kept, grad):
    return (low(grad),)
low.defvjp(low_keep, low_pass)
low_back.defvjp(back_keep, back_low)
HIGH = lax.Precision.HIGHEST
EPS = 1e-06
NEG = -1e+30

def matmul_high(left, right):
    return jnp.dot(left, right, precision=HIGH)

def rms_norm(values, gain):
    return values * lax.rsqrt(lax.optimization_barrier(jnp.mean(values * values, axis=-1, keepdims=True)) + EPS) * gain

def position_bias(rel_table, offset_bucket):
    picked = rel_table[offset_bucket]
    where = (jnp.arange(LEN, dtype=jnp.int32)[None, :] - jnp.arange(LEN, dtype=jnp.int32)[:, None] + LEN - 1).astype(jnp.int32)
    return jnp.transpose(picked[where], (2, 0, 1))

def slot_of(routes, capacity_keep):
    chosen = routes[:, 0].astype(jnp.int32)
    picked = (chosen[:, None] == jnp.arange(EXPERTS, dtype=jnp.int32)[None, :]).astype(jnp.int32)
    blocks = picked.reshape(DEVICES, TOK_DEV, EXPERTS)
    earlier = (jnp.cumsum(blocks, axis=1) - blocks).reshape(TOKENS, EXPERTS)
    ranking = lax.optimization_barrier(jnp.sum(earlier * picked, axis=-1)).astype(jnp.int32)
    block_index = (jnp.arange(TOKENS, dtype=jnp.int32) // TOK_DEV).astype(jnp.int32)
    slots = (chosen * (DEVICES * CAP) + block_index * CAP + ranking).astype(jnp.int32)
    outside = jnp.full_like(slots, EXPERTS * DEVICES * CAP)
    return (chosen, jnp.where(capacity_keep == 1, slots, outside).astype(jnp.int32))

def forward(inputs, gain_attn, gain_ffn, w_query, w_key, w_value, w_output, rel_table, router, expert_in, expert_out, segment_ids, offset_bucket, chosen, slots):
    scaling = HEAD_DIM ** (-0.5)
    normed = low(rms_norm(inputs, gain_attn))
    query = low_back(low(matmul_high(normed, w_query))).reshape(SEQS, LEN, HEADS, HEAD_DIM)
    keys = low_back(low(matmul_high(normed, w_key))).reshape(SEQS, LEN, HEADS, HEAD_DIM)
    values = low_back(low(matmul_high(normed, w_value))).reshape(SEQS, LEN, HEADS, HEAD_DIM)
    bias = position_bias(rel_table, offset_bucket)

    def one_sequence(item):
        q_seq, k_seq, v_seq, seg_seq = item
        score = jnp.einsum('qhd,khd->hqk', q_seq, k_seq, precision=HIGH) * scaling + bias
        score = low_back(score)
        same = seg_seq[:, None] == seg_seq[None, :]
        score = jnp.where(same[None], score, NEG)
        weights = low(jax.nn.softmax(score, axis=-1))
        return jnp.einsum('hqk,khd->qhd', weights, v_seq, precision=HIGH)
    mixed = lax.map(jax.checkpoint(one_sequence), (query, keys, values, segment_ids))
    mixed = low_back(low(mixed.reshape(TOKENS, HEADS * HEAD_DIM)))
    resid = inputs + low_back(matmul_high(mixed, w_output))
    normed_two = low(rms_norm(resid, gain_ffn))
    logits = low_back(matmul_high(normed_two, router))
    probs = jax.nn.softmax(logits, axis=-1)
    onehot = (chosen[:, None] == jnp.arange(EXPERTS, dtype=jnp.int32)[None, :]).astype(jnp.float32)
    gate = lax.optimization_barrier(jnp.sum(probs * onehot, axis=-1))
    entering = low_back(normed_two)
    buffer = jnp.zeros((EXPERTS * DEVICES * CAP, D), jnp.float32).at[slots].add(entering, mode='drop')
    buffer = buffer.reshape(EXPERTS, DEVICES * CAP, D)

    def one_expert(item):
        slot_rows, first, second = item
        hidden = low_back(matmul_high(slot_rows, first))
        active = low(jax.nn.gelu(hidden, approximate=True))
        return low_back(low(matmul_high(active, second)))
    result = lax.map(jax.checkpoint(one_expert), (buffer, expert_in, expert_out)).reshape(EXPERTS * DEVICES * CAP, D)
    back = jnp.take(result, slots, axis=0, mode='fill', fill_value=0.0)
    return resid + gate[:, None] * back

def reference(tokens, segment_ids, offset_bucket, routes, capacity_keep, gain_attn, gain_ffn, w_query, w_key, w_value, w_output, rel_table, router, expert_in, expert_out, grad_out):
    chosen, slots = slot_of(routes, capacity_keep)
    floats = [item.astype(jnp.float32) for item in (tokens, gain_attn, gain_ffn, w_query, w_key, w_value, w_output, rel_table, router, expert_in, expert_out)]

    def tied(*given):
        return forward(*given, segment_ids, offset_bucket, chosen, slots)
    output, pull = jax.vjp(tied, *floats)
    grads = pull(grad_out.astype(jnp.float32))
    return (output.astype(jnp.bfloat16), grads[0].astype(jnp.bfloat16), grads[1], grads[2], grads[3], grads[4], grads[5], grads[6], grads[7], grads[8], grads[9], grads[10])
```

```python
import functools

import jax
import jax.numpy as jnp
from jax import lax
from jax.experimental import pallas as pl
from jax.experimental.pallas import tpu as pltpu
from jax.sharding import PartitionSpec as P

F32=jnp.float32; BF=jnp.bfloat16
ROWS=256
def dot_t(a,b):
    return lax.dot_general(a,b,(((1,),(1,)),((),())),preferred_element_type=F32)
def dot_n(a,b):
    return lax.dot_general(a,b,(((1,),(0,)),((),())),preferred_element_type=F32)

def attn_fwd_kernel(scaling, head, q_ref,k_ref,v_ref,sq_ref,sk_ref,off_ref,o_ref,p_ref,bias):
    length=q_ref.shape[0]; wide=off_ref.shape[-1]
    lane=lax.broadcasted_iota(jnp.int32,(1,2*head),1)
    kext=jnp.concatenate([k_ref[...],sk_ref[...]],axis=1)
    outs=[None]*(length//ROWS)
    for hh in range(2):
        mine=(lane>=head*hh)&(lane<head*(hh+1))
        spread=jnp.broadcast_to(off_ref[0,hh:hh+1,:],(ROWS,wide))
        bias[...]=pltpu.roll(spread,wide-(ROWS-1),1,stride=1,stride_axis=0)
        for b in range(length//ROWS):
            rows=pl.ds(b*ROWS,ROWS)
            qm=jnp.where(mine,q_ref[rows,:].astype(F32)*scaling,0.0).astype(BF)
            s=dot_t(jnp.concatenate([qm,sq_ref[rows,:]],axis=1),kext)
            s=s+bias[:,length-ROWS-b*ROWS:2*length-ROWS-b*ROWS]
            m=jnp.max(s,axis=-1,keepdims=True)
            e=jnp.exp(s-m)
            inv=1.0/jnp.sum(e,axis=-1,keepdims=True)
            p=(e*inv).astype(BF)
            p_ref[0,hh,rows,:]=p
            o=dot_n(p,v_ref[...])
            if hh==0: outs[b]=o
            else: o_ref[rows,:]=jnp.where(mine,o,outs[b]).astype(BF)

def attn_fwd(qkv,sq,sk,off,heads,head):
    length=qkv.shape[0]; pairs=heads//2
    wide=off.shape[-1]
    return pl.pallas_call(functools.partial(attn_fwd_kernel,head**-0.5,head),
        grid=(pairs,),
        in_specs=[pl.BlockSpec((length,2*head),lambda p:(0,p)),
                  pl.BlockSpec((length,2*head),lambda p:(0,pairs+p)),
                  pl.BlockSpec((length,2*head),lambda p:(0,2*pairs+p)),
                  pl.BlockSpec((length,128),lambda p:(0,0)),
                  pl.BlockSpec((length,128),lambda p:(0,0)),
                  pl.BlockSpec((1,2,wide),lambda p:(p,0,0))],
        out_specs=[pl.BlockSpec((length,2*head),lambda p:(0,p)),
                   pl.BlockSpec((1,2,length,length),lambda p:(p,0,0,0))],
        out_shape=[jax.ShapeDtypeStruct((length,heads*head),BF),jax.ShapeDtypeStruct((pairs,2,length,length),BF)],
        scratch_shapes=[pltpu.VMEM((ROWS,wide),F32)],
        compiler_params=pltpu.CompilerParams(vmem_limit_bytes=56*2**20),
        name="attn_fwd",
    )(qkv,qkv,qkv,sq,sk,off)

def attn_bwd_kernel(scaling, head, q_ref,k_ref,v_ref,do_ref,o_ref,p_ref,dq_ref,dk_ref,dv_ref,doff_ref,acc):
    length=q_ref.shape[0]; wide=acc.shape[-1]
    lane=lax.broadcasted_iota(jnp.int32,(1,2*head),1)
    extra=jnp.where(lax.broadcasted_iota(jnp.int32,(length,128),1)<2,1.0,0.0).astype(BF)
    vext=jnp.concatenate([v_ref[...],extra],axis=1)
    lane_b=lax.broadcasted_iota(jnp.int32,(ROWS,128),1)
    dqs=[None]*(length//ROWS)
    dks=[];dvs=[]
    for hh in range(2):
        mine=(lane>=head*hh)&(lane<head*(hh+1))
        acc[...]=jnp.zeros_like(acc)
        dk=jnp.zeros((head,length),F32); dv=jnp.zeros((head,length),F32)
        for b in range(length//ROWS):
            rows=pl.ds(b*ROWS,ROWS)
            do=do_ref[rows,:]
            dom=jnp.where(mine,do.astype(F32),0.0)
            delta=-jnp.sum(dom*o_ref[rows,:].astype(F32),axis=-1,keepdims=True)
            hi=delta.astype(BF).astype(F32)
            ext=jnp.where(lane_b==0,hi,jnp.where(lane_b==1,delta-hi,0.0)).astype(BF)
            dp=dot_t(jnp.concatenate([dom.astype(BF),ext],axis=1),vext)
            p=p_ref[0,hh,rows,:]
            ds=p.astype(F32)*dp
            at=length-ROWS-b*ROWS
            acc[:,at:at+length]+=ds
            dsb=ds.astype(BF)
            dq=dot_n(dsb,k_ref[...])
            if hh==0: dqs[b]=dq
            else: dq_ref[rows,:]=(jnp.where(mine,dq,dqs[b])*scaling).astype(BF)
            qt=q_ref[rows,:].T[hh*head:(hh+1)*head]
            dot_=do.T[hh*head:(hh+1)*head]
            dk+=dot_n(qt,dsb)
            dv+=dot_n(dot_,p)
        dks.append(dk); dvs.append(dv)
        x=acc[...]
        n=ROWS
        while n>8:
            n//=2
            x=x[:n]+pltpu.roll(x[n:],wide-n,1)
        row=lax.broadcasted_iota(jnp.int32,x.shape,0)
        for bit in (4,2,1):
            x=jnp.where((row&bit)!=0,pltpu.roll(x,wide-bit,1),x)
        doff_ref[0,hh:hh+1,:]=pltpu.roll(jnp.broadcast_to(jnp.sum(x,axis=0,keepdims=True),(8,wide)),ROWS-1,1)[:1]
    dk_ref[...]=(jnp.concatenate(dks,axis=0).T*scaling).astype(BF)
    dv_ref[...]=jnp.concatenate(dvs,axis=0).T.astype(BF)

def attn_bwd(qkv,do,o,p,wide,heads,head):
    length=qkv.shape[0]; pairs=heads//2
    col=lambda at: pl.BlockSpec((length,2*head),lambda p:(0,at+p))
    return pl.pallas_call(functools.partial(attn_bwd_kernel,head**-0.5,head),
        grid=(pairs,),
        in_specs=[col(0),col(pairs),col(2*pairs),col(0),col(0),
                  pl.BlockSpec((1,2,length,length),lambda p:(p,0,0,0))],
        out_specs=[col(0),col(0),col(0),pl.BlockSpec((1,2,wide),lambda p:(p,0,0))],
        out_shape=[jax.ShapeDtypeStruct((length,heads*head),BF)]*3+[jax.ShapeDtypeStruct((pairs,2,wide),F32)],
        scratch_shapes=[pltpu.VMEM((ROWS,wide),F32)],
        compiler_params=pltpu.CompilerParams(vmem_limit_bytes=56*2**20),
        name="attn_bwd",
    )(qkv,qkv,qkv,do,o,p)
FB=512
def gelu_pair(u):
    c=0.7978845608028654
    sq=u*u
    t=jnp.tanh(c*(u+0.044715*(u*sq)))
    half=0.5*(1.0+t)
    return u*half, half+0.5*u*(1.0-t*t)*(c+(3.0*0.044715*c)*sq)

def expert_kernel(experts,x_ref,g_ref,router_ref,mine_ref,win_ref,wout_ref,
                  geo_ref,dn_ref,act_ref,du_ref,deo_ref,drouter_ref,eo,dx,gate):
    step=pl.program_id(0); last=pl.num_programs(0)-1
    def probabilities():
        logits=dot_n(x_ref[...],router_ref[...])
        lane=lax.broadcasted_iota(jnp.int32,logits.shape,1)
        logits=jnp.where(lane<experts,logits,-1e30)
        e=jnp.exp(logits-jnp.max(logits,axis=-1,keepdims=True))
        return e/jnp.sum(e,axis=-1,keepdims=True)
    @pl.when(step==0)
    def _():
        chosen=jnp.sum(probabilities()*mine_ref[...],axis=-1,keepdims=True)
        gate[...]=jnp.broadcast_to(chosen,gate.shape)
        deo_ref[...]=(chosen*g_ref[...].astype(F32)).astype(BF)
        eo[...]=jnp.zeros_like(eo); dx[...]=jnp.zeros_like(dx)
    u=dot_n(x_ref[...],win_ref[0])
    dact=dot_t(deo_ref[...],wout_ref[0])
    a,slope=gelu_pair(u)
    a=a.astype(BF)
    d=(dact*slope).astype(BF)
    act_ref[...]=a; du_ref[...]=d
    eo[...]+=dot_n(a,wout_ref[0])
    dx[...]+=dot_t(d,win_ref[0])
    @pl.when(step==last)
    def _():
        made=eo[...].astype(BF).astype(F32)
        chosen=gate[:,:1]
        geo_ref[...]=(chosen*made).astype(BF)
        dgate=jnp.sum(made*g_ref[...].astype(F32),axis=-1,keepdims=True)
        probs=probabilities()
        dprobs=mine_ref[...]*dgate
        dlog=(probs*(dprobs-jnp.sum(probs*dprobs,axis=-1,keepdims=True))).astype(BF)
        dn_ref[...]=(dx[...]+dot_t(dlog,router_ref[...])).astype(BF)
        drouter_ref[...]=dot_n(dlog.T,x_ref[...])

def expert(x,g,router,mine,win,wout,experts):
    rows,width=x.shape; ff=win.shape[-1]
    fixed=lambda shape: pl.BlockSpec(shape,lambda f:(0,)*len(shape))
    return pl.pallas_call(functools.partial(expert_kernel,experts),
        grid=(ff//FB,),
        in_specs=[fixed((rows,width)),fixed((rows,width)),fixed((width,128)),fixed((1,128)),
                  pl.BlockSpec((1,width,FB),lambda f:(0,0,f)),pl.BlockSpec((1,FB,width),lambda f:(0,f,0))],
        out_specs=[fixed((rows,width)),fixed((rows,width)),pl.BlockSpec((rows,FB),lambda f:(0,f)),
                   pl.BlockSpec((rows,FB),lambda f:(0,f)),fixed((rows,width)),fixed((128,width))],
        out_shape=[jax.ShapeDtypeStruct((rows,width),BF),jax.ShapeDtypeStruct((rows,width),BF),
                   jax.ShapeDtypeStruct((rows,ff),BF),jax.ShapeDtypeStruct((rows,ff),BF),
                   jax.ShapeDtypeStruct((rows,width),BF),jax.ShapeDtypeStruct((128,width),F32)],
        scratch_shapes=[pltpu.VMEM((rows,width),F32),pltpu.VMEM((rows,width),F32),pltpu.VMEM((rows,128),F32)],
        compiler_params=pltpu.CompilerParams(vmem_limit_bytes=56*2**20),
        cost_estimate=pl.CostEstimate(flops=8*rows*width*ff,bytes_accessed=4*width*ff+4*rows*ff,transcendentals=rows*ff),
        name="expert",
    )(x,g,router,mine,win,wout)

def weights_kernel(parts,*refs):
    xs,deos,acts,dus=(refs[i*parts:(i+1)*parts] for i in range(4))
    din_ref,dout_ref=refs[4*parts:4*parts+2]; turned=refs[4*parts+2:]
    @pl.when(pl.program_id(0)==0)
    def _():
        for t,x in zip(turned,xs): t[...]=x[...].T
    din=dout=None
    for t,deo,act,du in zip(turned,deos,acts,dus):
        a=dot_n(t[...],du[...])
        b=lax.dot_general(act[...],deo[...],(((0,),(0,)),((),())),preferred_element_type=F32)
        din=a if din is None else din+a
        dout=b if dout is None else dout+b
    din_ref[...]=din.astype(din_ref.dtype)
    dout_ref[...]=dout.astype(dout_ref.dtype)

def expert_weights(xs,deos,acts,dus,kind):
    width=xs[0].shape[1]; ff=acts[0].shape[1]; parts=len(xs)
    total=sum(x.shape[0] for x in xs)
    fixed=lambda shape: pl.BlockSpec(shape,lambda f:(0,)*len(shape))
    return pl.pallas_call(functools.partial(weights_kernel,parts),
        grid=(ff//FB,),
        in_specs=[fixed(x.shape) for x in xs]+[fixed(x.shape) for x in deos]
                 +[pl.BlockSpec((a.shape[0],FB),lambda f:(0,f)) for a in acts]
                 +[pl.BlockSpec((a.shape[0],FB),lambda f:(0,f)) for a in dus],
        out_specs=[pl.BlockSpec((width,FB),lambda f:(0,f)),pl.BlockSpec((FB,width),lambda f:(f,0))],
        out_shape=[jax.ShapeDtypeStruct((width,ff),kind),jax.ShapeDtypeStruct((ff,width),kind)],
        scratch_shapes=[pltpu.VMEM((width,x.shape[0]),BF) for x in xs],
        compiler_params=pltpu.CompilerParams(vmem_limit_bytes=56*2**20),
        cost_estimate=pl.CostEstimate(flops=4*total*width*ff,bytes_accessed=4*width*ff+4*total*ff,transcendentals=0),
        name="expert_weights",
    )(*xs,*deos,*acts,*dus)
EPS = 1e-06
NEG = -1e30
HIGH = lax.Precision.HIGHEST
GROUP = ("fsdp", "expert")


def normalize(values, gain):
    row_scale = lax.rsqrt(jnp.mean(values * values, axis=-1, keepdims=True) + EPS)
    return (values * row_scale * gain, row_scale)


def normalize_back(values, row_scale, gain, cotangent):
    weighted = cotangent * gain
    d_gain = jnp.sum(cotangent * values * row_scale, axis=0)
    d_values = row_scale * weighted - values * row_scale**3 * jnp.mean(
        weighted * values, axis=-1, keepdims=True
    )
    return (d_values, d_gain)


def dot32(left, right):
    return jnp.dot(left, right, preferred_element_type=F32)


def swap(blocks, sign, experts):
    moved = [
        lax.ppermute(block, "expert", [(i, (i + sign * (at + 1)) % experts) for i in range(experts)])
        for at, block in enumerate(blocks)
    ]
    return moved


def after(value, earlier):
    return lax.optimization_barrier((value, earlier))[0]


def body(
    group_size,
    tokens,
    segment_ids,
    offset_bucket,
    routes,
    capacity_keep,
    gain_attn,
    gain_ffn,
    w_query,
    w_key,
    w_value,
    w_output,
    rel_table,
    router,
    expert_in,
    expert_out,
    grad_out,
):
    length = segment_ids.shape[1]
    heads = rel_table.shape[1]
    inner = w_query.shape[1]
    head = inner // heads
    experts = router.shape[1]
    token_rows, width = tokens.shape
    capacity = token_rows * 5 // (4 * experts)
    slots = experts * capacity
    shard = w_query.shape[0]
    own_buckets = rel_table.shape[0]
    buckets = own_buckets * group_size
    me = lax.axis_index("expert")

    small_cols = [
        gain_attn[:, None],
        gain_ffn[:, None],
        router,
        jnp.pad(rel_table, ((0, shard - own_buckets), (0, 0))),
    ]
    used = 2 + experts + heads
    packed = jnp.concatenate(
        [w_query, w_key, w_value] + small_cols + [jnp.zeros((shard, -used % 128), BF)], axis=1
    )
    gathered = lax.all_gather(packed, GROUP, axis=0, tiled=True)
    proj_in = gathered[:, : 3 * inner]
    small = gathered[:, 3 * inner :]
    gain_one = small[:, 0].astype(F32)
    gain_two = small[:, 1].astype(F32)
    route_weight = small[:, 2 : 2 + experts]
    table = small[:, 2 + experts : used].reshape(group_size, shard, heads)[:, :own_buckets]
    table = table.reshape(buckets, heads)
    proj_output = lax.all_gather(after(w_output, gathered), GROUP, axis=0, tiled=True)

    chosen = routes[:, 0]
    picked = (chosen[:, None] == jnp.arange(experts, dtype=jnp.int32)[None, :]).astype(jnp.int32)
    earlier = jnp.cumsum(picked, axis=0) - picked
    slot = lax.rem(chosen - me + experts, experts) * capacity + jnp.sum(earlier * picked, axis=-1)
    slot = jnp.where(capacity_keep == 1, slot, slots)
    slot_ids = jnp.arange(slots, dtype=jnp.int32)
    to_slots = (slot_ids[:, None] == slot[None, :]).astype(BF)
    to_tokens = (slot[:, None] == slot_ids[None, :]).astype(BF)

    def leave(values, first, last):
        return dot32(to_slots[first:last], values).astype(BF)

    def depart(values):
        return [leave(values, s * capacity, (s + 1) * capacity) for s in range(1, experts)]

    g_local = leave(grad_out, 0, capacity)
    g_remote = jnp.concatenate(
        swap([after(block, gathered) for block in depart(grad_out)], 1, experts), axis=0
    )

    inputs = tokens.astype(F32)
    normed, scale_one = normalize(inputs, gain_one)
    normed_low = normed.astype(BF)
    qkv = dot32(normed_low, proj_in).astype(BF)

    bucket_of = jnp.concatenate([offset_bucket, jnp.full((1,), -1, jnp.int32)])
    hits = (bucket_of[None, :] == jnp.arange(buckets, dtype=jnp.int32)[:, None]).astype(BF)
    offsets = dot32(table.T, hits).reshape(heads // 2, 2, 2 * length)
    same = segment_ids[0][:, None] == jnp.arange(128, dtype=jnp.int32)[None, :]
    seg_q = jnp.where(same, 0.0, NEG).astype(BF)
    seg_k = same.astype(BF)
    attn_out, weights = attn_fwd(qkv, seg_q, seg_k, offsets, heads, head)

    resid = inputs + dot32(attn_out, proj_output)
    normed_two, scale_two = normalize(resid, gain_two)
    second_low = normed_two.astype(BF)

    x_remote = jnp.concatenate(swap(depart(second_low), 1, experts), axis=0)
    x_local = leave(second_low, 0, capacity)
    route_wide = jnp.pad(route_weight, ((0, 0), (0, 128 - experts)))
    mine = (jnp.arange(128, dtype=jnp.int32) == me).astype(F32)[None, :]
    geo_l, dn_l, act_l, du_l, deo_l, dr_l = expert(
        x_local, g_local, route_wide, mine, expert_in, expert_out, experts
    )
    geo_r, dn_r, act_r, du_r, deo_r, dr_r = expert(
        x_remote, g_remote, route_wide, mine, expert_in, expert_out, experts
    )

    def cut(rows):
        return [rows[s * capacity : (s + 1) * capacity] for s in range(experts - 1)]

    dn_back = swap(cut(dn_r), -1, experts)
    d_in, d_out = expert_weights([x_local, x_remote], [deo_l, deo_r], [act_l, act_r], [du_l, du_r], BF)
    sum_in, sum_out = lax.psum((d_in, d_out), ("rep", "fsdp"))
    d_second = dot32(to_tokens, jnp.concatenate([dn_l] + dn_back, axis=0))
    geo_back = swap(cut(after(geo_r, dn_back[-1])), -1, experts)
    output = resid + dot32(to_tokens, jnp.concatenate([geo_l] + geo_back, axis=0))
    output = output.astype(BF)
    d_router = (dr_l + dr_r)[:experts].T

    cotangent = grad_out.astype(F32)
    d_resid_norm, d_gain_two = normalize_back(resid, scale_two, gain_two, d_second)
    d_resid = cotangent + d_resid_norm
    d_branch = d_resid.astype(BF)
    d_attn = dot_t(d_branch, proj_output).astype(BF)
    d_proj_output = lax.dot_general(
        attn_out, d_branch, (((0,), (0,)), ((), ())), preferred_element_type=F32
    ).astype(BF)
    d_query, d_key, d_value, d_offsets = attn_bwd(
        qkv, d_attn, attn_out, weights, 2 * length, heads, head
    )
    d_table = jnp.dot(
        hits.astype(F32), d_offsets.reshape(heads, 2 * length).T, precision=HIGH
    )
    d_qkv = jnp.concatenate([d_query, d_key, d_value], axis=1)
    d_proj = lax.dot_general(
        normed_low, d_qkv, (((0,), (0,)), ((), ())), preferred_element_type=F32
    ).astype(BF)
    d_normed = dot_t(d_qkv, proj_in)
    d_input_norm, d_gain_one = normalize_back(inputs, scale_one, gain_one, d_normed)
    grad_tokens = (d_resid + d_input_norm).astype(BF)

    share_out = lax.psum_scatter(d_proj_output, GROUP, scatter_dimension=0, tiled=True)
    share_in = lax.psum_scatter(d_proj, GROUP, scatter_dimension=0, tiled=True)
    d_small = jnp.concatenate(
        [
            d_gain_one[:, None],
            d_gain_two[:, None],
            d_router,
            jnp.pad(
                d_table.reshape(group_size, own_buckets, heads),
                ((0, 0), (0, shard - own_buckets), (0, 0)),
            ).reshape(width, heads),
            jnp.zeros((width, -used % 128), F32),
        ],
        axis=1,
    )
    share_small = lax.psum_scatter(d_small, GROUP, scatter_dimension=0, tiled=True)
    share_out, share_in, share_small = lax.psum((share_out, share_in, share_small), "rep")
    share_in = share_in.astype(F32)
    return (
        output,
        grad_tokens,
        share_small[:, 0],
        share_small[:, 1],
        share_in[:, :inner],
        share_in[:, inner : 2 * inner],
        share_in[:, 2 * inner :],
        share_out.astype(F32),
        share_small[:own_buckets, 2 + experts : used],
        share_small[:, 2 : 2 + experts],
        sum_in.astype(F32)[None],
        sum_out.astype(F32)[None],
    )


def solution(mesh):
    rows, group = P(("rep", "fsdp", "expert"), None), P(("fsdp", "expert"), None)
    flat_rows, flat_group = P(("rep", "fsdp", "expert")), P(("fsdp", "expert"))
    whole = P("expert", None, None)
    group_size = mesh.shape["fsdp"] * mesh.shape["expert"]
    return jax.shard_map(
        functools.partial(body, group_size),
        mesh=mesh,
        in_specs=(
            rows, rows, P(), rows, flat_rows, flat_group, flat_group,
            group, group, group, group, group, group, whole, whole, rows,
        ),
        out_specs=(
            rows, rows, flat_group, flat_group,
            group, group, group, group, group, group, whole, whole,
        ),
        check_vma=False,
    )
```

```python
import functools

import jax
import jax.numpy as jnp
from jax import lax
from jax.experimental import pallas as pl
from jax.experimental.pallas import tpu as pltpu
from jax.sharding import PartitionSpec as P

F32 = jnp.float32
BF = jnp.bfloat16
ROWS = 512
TILE = 128
VMEM_BYTES = 56 * 2**20


def dot_t(a, b):
    return lax.dot_general(a, b, (((1,), (1,)), ((), ())), preferred_element_type=F32)


def dot_n(a, b):
    return lax.dot_general(a, b, (((1,), (0,)), ((), ())), preferred_element_type=F32)


def skew(row, wide, out_ref):
    x = pltpu.roll(jnp.broadcast_to(row, (8, wide)), wide - (TILE - 1), 1)
    index = lax.broadcasted_iota(jnp.int32, x.shape, 0)
    for bit in (1, 2, 4):
        x = jnp.where((index & bit) != 0, pltpu.roll(x, bit, 1), x)
    n = 8
    while n < TILE:
        x = jnp.concatenate([x, pltpu.roll(x, n, 1)], axis=0)
        n *= 2
    out_ref[...] = x


def unskew(x, wide):
    n = x.shape[0]
    while n > 8:
        n //= 2
        x = x[:n] + pltpu.roll(x[n:], wide - n, 1)
    index = lax.broadcasted_iota(jnp.int32, x.shape, 0)
    for bit in (4, 2, 1):
        x = jnp.where((index & bit) != 0, pltpu.roll(x, wide - bit, 1), x)
    total = jnp.broadcast_to(jnp.sum(x, axis=0, keepdims=True), (8, wide))
    return pltpu.roll(total, TILE - 1, 1)[:1]


def attn_fwd_kernel(
    scaling, head, q_ref, k_ref, v_ref, sq_ref, sk_ref, off_ref, o_ref, inv_ref, e_ref, bias0, bias1
):
    length = q_ref.shape[0]
    wide = off_ref.shape[-1]
    lane = lax.broadcasted_iota(jnp.int32, (1, 2 * head), 1)
    firsts = lane < head
    bias = (bias0, bias1)
    for hh in range(2):
        skew(off_ref[0, hh : hh + 1, :], wide, bias[hh])
    kx = jnp.concatenate([k_ref[...], sk_ref[...]], axis=1)
    vx = v_ref[...]
    for b in range(length // ROWS):
        rows = pl.ds(b * ROWS, ROWS)
        q = q_ref[rows, :].astype(F32) * scaling
        made = []
        for hh in range(2):
            mine = firsts if hh == 0 else jnp.logical_not(firsts)
            qx = jnp.concatenate([jnp.where(mine, q, 0.0).astype(BF), sq_ref[rows, :]], axis=1)
            tiles = []
            for a in range(ROWS // TILE):
                at = length - TILE * (1 + a) - b * ROWS
                tiles.append(bias[hh][:, at : at + length])
            s = dot_t(qx, kx) + jnp.concatenate(tiles, axis=0)
            e = jnp.exp(s - jnp.max(s, axis=-1, keepdims=True)).astype(BF)
            e_ref[0, hh, rows, :] = e
            made.append(dot_n(e, jnp.where(mine, vx, jnp.ones_like(vx))))
        sums = jnp.where(firsts, pltpu.roll(made[0], head, 1), pltpu.roll(made[1], head, 1))
        inv = 1.0 / sums
        inv_ref[rows, :] = inv
        o_ref[rows, :] = (jnp.where(firsts, made[0], made[1]) * inv).astype(BF)


def attn_fwd(qkv, sq, sk, off, heads, head):
    length = qkv.shape[0]
    pairs = heads // 2
    wide = off.shape[-1]
    col = lambda at: pl.BlockSpec((length, 2 * head), lambda p: (0, at + p))
    fixed = pl.BlockSpec((length, 128), lambda p: (0, 0))
    return pl.pallas_call(
        functools.partial(attn_fwd_kernel, head**-0.5, head),
        grid=(pairs,),
        in_specs=[
            col(0), col(pairs), col(2 * pairs), fixed, fixed,
            pl.BlockSpec((1, 2, wide), lambda p: (p, 0, 0)),
        ],
        out_specs=[col(0), col(0), pl.BlockSpec((1, 2, length, length), lambda p: (p, 0, 0, 0))],
        out_shape=[
            jax.ShapeDtypeStruct((length, heads * head), BF),
            jax.ShapeDtypeStruct((length, heads * head), F32),
            jax.ShapeDtypeStruct((pairs, 2, length, length), BF),
        ],
        scratch_shapes=[pltpu.VMEM((TILE, wide), F32)] * 2,
        compiler_params=pltpu.CompilerParams(vmem_limit_bytes=VMEM_BYTES),
        cost_estimate=pl.CostEstimate(
            flops=40 * heads * length * length * head // 2,
            bytes_accessed=2 * heads * length * length,
            transcendentals=heads * length * length,
        ),
        name="attn_fwd",
    )(qkv, qkv, qkv, sq, sk, off)


def attn_bwd_kernel(
    scaling, head, q_ref, k_ref, v_ref, do_ref, o_ref, inv_ref, e_ref,
    dq_ref, dk_ref, dv_ref, doff_ref, acc0, acc1, dkt, dvt,
):
    length = q_ref.shape[0]
    wide = acc0.shape[-1]
    lane = lax.broadcasted_iota(jnp.int32, (1, 2 * head), 1)
    firsts = lane < head
    acc = (acc0, acc1)
    for ref in (acc0, acc1, dkt, dvt):
        ref[...] = jnp.zeros_like(ref)
    lane_b = lax.broadcasted_iota(jnp.int32, (ROWS, 128), 1)
    extra = jnp.where(lax.broadcasted_iota(jnp.int32, (length, 128), 1) < 2, 1.0, 0.0).astype(BF)
    vx = jnp.concatenate([v_ref[...], extra], axis=1)
    kx = k_ref[...]
    for b in range(length // ROWS):
        rows = pl.ds(b * ROWS, ROWS)
        do = do_ref[rows, :].astype(F32) * inv_ref[rows, :]
        toward = do * o_ref[rows, :].astype(F32)
        qt = q_ref[rows, :].T
        dot = do.astype(BF).T
        made = []
        for hh in range(2):
            mine = firsts if hh == 0 else jnp.logical_not(firsts)
            part = slice(hh * head, (hh + 1) * head)
            delta = -jnp.sum(jnp.where(mine, toward, 0.0), axis=-1, keepdims=True)
            hi = delta.astype(BF).astype(F32)
            ext = jnp.where(lane_b == 0, hi, jnp.where(lane_b == 1, delta - hi, 0.0)).astype(BF)
            dp = dot_t(jnp.concatenate([jnp.where(mine, do, 0.0).astype(BF), ext], axis=1), vx)
            e = e_ref[0, hh, rows, :]
            ds = e.astype(F32) * dp
            for a in range(ROWS // TILE):
                at = length - TILE * (1 + a) - b * ROWS
                acc[hh][:, at : at + length] += ds[a * TILE : (a + 1) * TILE]
            low = ds.astype(BF)
            made.append(dot_n(low, kx))
            dkt[part, :] += dot_n(qt[part], low)
            dvt[part, :] += dot_n(dot[part], e)
        dq_ref[rows, :] = (jnp.where(firsts, made[0], made[1]) * scaling).astype(BF)
    for hh in range(2):
        doff_ref[0, hh : hh + 1, :] = unskew(acc[hh][...], wide)
    dk_ref[...] = (dkt[...].T * scaling).astype(BF)
    dv_ref[...] = dvt[...].T.astype(BF)


def attn_bwd(qkv, do, o, inv, e, wide, heads, head):
    length = qkv.shape[0]
    pairs = heads // 2
    col = lambda at: pl.BlockSpec((length, 2 * head), lambda p: (0, at + p))
    return pl.pallas_call(
        functools.partial(attn_bwd_kernel, head**-0.5, head),
        grid=(pairs,),
        in_specs=[
            col(0), col(pairs), col(2 * pairs), col(0), col(0), col(0),
            pl.BlockSpec((1, 2, length, length), lambda p: (p, 0, 0, 0)),
        ],
        out_specs=[col(0), col(0), col(0), pl.BlockSpec((1, 2, wide), lambda p: (p, 0, 0))],
        out_shape=[jax.ShapeDtypeStruct((length, heads * head), BF)] * 3
        + [jax.ShapeDtypeStruct((pairs, 2, wide), F32)],
        scratch_shapes=[pltpu.VMEM((TILE, wide), F32)] * 2
        + [pltpu.VMEM((2 * head, length), F32)] * 2,
        compiler_params=pltpu.CompilerParams(vmem_limit_bytes=VMEM_BYTES),
        cost_estimate=pl.CostEstimate(
            flops=40 * heads * length * length * head // 2,
            bytes_accessed=2 * heads * length * length,
            transcendentals=0,
        ),
        name="attn_bwd",
    )(qkv, qkv, qkv, do, o, inv, e)
FF_BLOCK = 512


def gelu_pair(u):
    c = 0.7978845608028654
    sq = u * u
    t = jnp.tanh(u * (c + (0.044715 * c) * sq))
    half = 0.5 + 0.5 * t
    return u * half, half + (0.5 * u) * (1.0 - t * t) * (c + (3.0 * 0.044715 * c) * sq)


def probabilities(x, router, experts):
    logits = dot_n(x, router)
    lane = lax.broadcasted_iota(jnp.int32, logits.shape, 1)
    logits = jnp.where(lane < experts, logits, -1e30)
    e = jnp.exp(logits - jnp.max(logits, axis=-1, keepdims=True))
    return e / jnp.sum(e, axis=-1, keepdims=True)


def hidden_step(x_ref, deo_ref, win_ref, wout_ref, act_ref, du_ref):
    win, wout = win_ref[0], wout_ref[0]
    rows = x_ref.shape[0]
    parts = 2 if rows % 32 == 0 else 1
    step = rows // parts
    for at in range(0, rows, step):
        part = pl.ds(at, step)
        u = dot_n(x_ref[part, :], win)
        dact = dot_t(deo_ref[part, :], wout)
        a, slope = gelu_pair(u)
        act_ref[part, :] = a.astype(BF)
        du_ref[part, :] = (dact * slope).astype(BF)


def gated_cotangent(experts, x_ref, g_ref, router_ref, mine_ref, deo_ref):
    probs = probabilities(x_ref[...], router_ref[...], experts)
    gate = jnp.sum(probs * mine_ref[...], axis=-1, keepdims=True)
    deo_ref[...] = (gate * g_ref[...].astype(F32)).astype(BF)


def hidden_kernel(
    experts, x_ref, g_ref, router_ref, mine_ref, win_ref, wout_ref, act_ref, du_ref, deo_ref
):
    @pl.when(pl.program_id(0) == 0)
    def _():
        gated_cotangent(experts, x_ref, g_ref, router_ref, mine_ref, deo_ref)

    hidden_step(x_ref, deo_ref, win_ref, wout_ref, act_ref, du_ref)


def fixed(*shape):
    return pl.BlockSpec(shape, lambda f: (0,) * len(shape))


def in_block(width):
    return pl.BlockSpec((1, width, FF_BLOCK), lambda f: (0, 0, f))


def out_block(width):
    return pl.BlockSpec((1, FF_BLOCK, width), lambda f: (0, f, 0))


def slot_block(rows):
    return pl.BlockSpec((rows, FF_BLOCK), lambda f: (0, f))


def expert_hidden(x, g, router, mine, win, wout, experts):
    rows, width = x.shape
    ff = win.shape[-1]
    return pl.pallas_call(
        functools.partial(hidden_kernel, experts),
        grid=(ff // FF_BLOCK,),
        in_specs=[
            fixed(rows, width), fixed(rows, width), fixed(width, 128), fixed(1, 128),
            in_block(width), out_block(width),
        ],
        out_specs=[slot_block(rows), slot_block(rows), fixed(rows, width)],
        out_shape=[
            jax.ShapeDtypeStruct((rows, ff), BF),
            jax.ShapeDtypeStruct((rows, ff), BF),
            jax.ShapeDtypeStruct((rows, width), BF),
        ],
        compiler_params=pltpu.CompilerParams(vmem_limit_bytes=VMEM_BYTES),
        cost_estimate=pl.CostEstimate(
            flops=8 * rows * width * ff,
            bytes_accessed=4 * width * ff + 4 * rows * ff,
            transcendentals=rows * ff,
        ),
        name="expert_hidden",
    )(x, g, router, mine, win, wout)


def gradients_kernel(
    experts, x_ref, g_ref, router_ref, mine_ref, win_ref, wout_ref, xl_ref, deol_ref, actl_ref,
    dul_ref, act_ref, du_ref, deo_ref, din_ref, dout_ref, xt, xlt,
):
    @pl.when(pl.program_id(0) == 0)
    def _():
        gated_cotangent(experts, x_ref, g_ref, router_ref, mine_ref, deo_ref)
        xt[...] = x_ref[...].T
        xlt[...] = xl_ref[...].T

    hidden_step(x_ref, deo_ref, win_ref, wout_ref, act_ref, du_ref)
    din_ref[...] = (dot_n(xlt[...], dul_ref[...]) + dot_n(xt[...], du_ref[...])).astype(BF)
    dout_ref[...] = (dot_n(actl_ref[...].T, deol_ref[...]) + dot_n(act_ref[...].T, deo_ref[...])).astype(BF)


def expert_gradients(x, g, router, mine, win, wout, x_local, deo_local, act_local, du_local, experts):
    rows, width = x.shape
    own = x_local.shape[0]
    ff = win.shape[-1]
    return pl.pallas_call(
        functools.partial(gradients_kernel, experts),
        grid=(ff // FF_BLOCK,),
        in_specs=[
            fixed(rows, width), fixed(rows, width), fixed(width, 128), fixed(1, 128),
            in_block(width), out_block(width), fixed(own, width), fixed(own, width),
            slot_block(own), slot_block(own),
        ],
        out_specs=[
            slot_block(rows), slot_block(rows), fixed(rows, width),
            pl.BlockSpec((width, FF_BLOCK), lambda f: (0, f)),
            pl.BlockSpec((FF_BLOCK, width), lambda f: (f, 0)),
        ],
        out_shape=[
            jax.ShapeDtypeStruct((rows, ff), BF),
            jax.ShapeDtypeStruct((rows, ff), BF),
            jax.ShapeDtypeStruct((rows, width), BF),
            jax.ShapeDtypeStruct((width, ff), BF),
            jax.ShapeDtypeStruct((ff, width), BF),
        ],
        scratch_shapes=[pltpu.VMEM((width, rows), BF), pltpu.VMEM((width, own), BF)],
        compiler_params=pltpu.CompilerParams(vmem_limit_bytes=VMEM_BYTES),
        cost_estimate=pl.CostEstimate(
            flops=12 * (rows + own) * width * ff,
            bytes_accessed=8 * width * ff + 4 * (rows + own) * ff,
            transcendentals=rows * ff,
        ),
        name="expert_gradients",
    )(x, g, router, mine, win, wout, x_local, deo_local, act_local, du_local)


def results_kernel(
    experts, x_ref, g_ref, router_ref, mine_ref, win_ref, wout_ref, act_ref, du_ref,
    geo_ref, dn_ref, drouter_ref, eo, dx,
):
    step = pl.program_id(0)

    @pl.when(step == 0)
    def _():
        eo[...] = dot_n(act_ref[...], wout_ref[0])
        dx[...] = dot_t(du_ref[...], win_ref[0])

    @pl.when(step > 0)
    def _():
        eo[...] += dot_n(act_ref[...], wout_ref[0])
        dx[...] += dot_t(du_ref[...], win_ref[0])

    @pl.when(step == pl.num_programs(0) - 1)
    def _():
        made = eo[...].astype(BF).astype(F32)
        mine = mine_ref[...]
        probs = probabilities(x_ref[...], router_ref[...], experts)
        gate = jnp.sum(probs * mine, axis=-1, keepdims=True)
        geo_ref[...] = (gate * made).astype(BF)
        dgate = jnp.sum(made * g_ref[...].astype(F32), axis=-1, keepdims=True)
        dprobs = mine * dgate
        dlog = probs * (dprobs - jnp.sum(probs * dprobs, axis=-1, keepdims=True))
        dlog = dlog.astype(BF)
        dn_ref[...] = (dx[...] + dot_t(dlog, router_ref[...])).astype(BF)
        drouter_ref[...] = dot_n(dlog.T, x_ref[...])


def expert_results(x, g, router, mine, win, wout, act, du, experts):
    rows, width = x.shape
    ff = win.shape[-1]
    return pl.pallas_call(
        functools.partial(results_kernel, experts),
        grid=(ff // FF_BLOCK,),
        in_specs=[
            fixed(rows, width), fixed(rows, width), fixed(width, 128), fixed(1, 128),
            in_block(width), out_block(width), slot_block(rows), slot_block(rows),
        ],
        out_specs=[fixed(rows, width), fixed(rows, width), fixed(128, width)],
        out_shape=[
            jax.ShapeDtypeStruct((rows, width), BF),
            jax.ShapeDtypeStruct((rows, width), BF),
            jax.ShapeDtypeStruct((128, width), F32),
        ],
        scratch_shapes=[pltpu.VMEM((rows, width), F32), pltpu.VMEM((rows, width), F32)],
        compiler_params=pltpu.CompilerParams(vmem_limit_bytes=VMEM_BYTES),
        cost_estimate=pl.CostEstimate(
            flops=8 * rows * width * ff,
            bytes_accessed=4 * width * ff + 4 * rows * ff,
            transcendentals=0,
        ),
        name="expert_results",
    )(x, g, router, mine, win, wout, act, du)
EPS = 1e-06
NEG = -1e30
HIGH = lax.Precision.HIGHEST
GROUP = ("fsdp", "expert")


def normalize(values, gain):
    row_scale = lax.rsqrt(jnp.mean(values * values, axis=-1, keepdims=True) + EPS)
    return (values * row_scale * gain, row_scale)


def normalize_back(values, row_scale, gain, cotangent):
    weighted = cotangent * gain
    d_gain = jnp.sum(cotangent * values * row_scale, axis=0)
    d_values = row_scale * weighted - values * row_scale**3 * jnp.mean(
        weighted * values, axis=-1, keepdims=True
    )
    return (d_values, d_gain)


def dot32(left, right):
    return jnp.dot(left, right, preferred_element_type=F32)


def bits_of(axis, size):
    return [(axis, size >> (k + 1)) for k in range(size.bit_length() - 1)]


def partner(value, key, sizes):
    axis, bit = key
    return lax.ppermute(value, axis, [(i, i ^ bit) for i in range(sizes[axis])])


def side(key):
    return lax.rem(lax.axis_index(key[0]) // key[1], 2)


def gather_bits(value, order, keys, sizes):
    held = []
    shape = value.shape
    for key in order:
        got = partner(value, key, sizes)
        at = sum(keys.index(other) < keys.index(key) for other in held)
        lower = side(key) == 0
        value = jnp.where(lower, jnp.stack([value, got], at), jnp.stack([got, value], at))
        held.append(key)
    return value.reshape((-1,) + shape[1:])


def scatter_bits(value, order, keys, sizes):
    held = list(keys)
    value = value.reshape((2,) * len(keys) + (value.shape[0] >> len(keys),) + value.shape[1:])
    for key in order:
        at = held.index(key)
        mine = side(key)
        got = partner(lax.dynamic_index_in_dim(value, 1 - mine, at, False), key, sizes)
        kept = lax.dynamic_index_in_dim(value, mine, at, False)
        value = (kept.astype(F32) + got.astype(F32)).astype(value.dtype)
        held.remove(key)
    return value


def shift(value, axis, by, size):
    return lax.ppermute(value, axis, [(i, (i + by) % size) for i in range(size)])


def sum_over(value, axis, size):
    me = lax.axis_index(axis)
    blocks = value.reshape((size, value.shape[0] // size) + value.shape[1:])
    total = lax.dynamic_index_in_dim(blocks, me, 0, False).astype(F32)
    for s in range(1, size):
        block = lax.dynamic_index_in_dim(blocks, lax.rem(me + s, size), 0, False)
        total = total + shift(block, axis, s, size).astype(F32)
    total = total.astype(value.dtype)
    out = lax.dynamic_update_index_in_dim(jnp.zeros_like(blocks), total, me, 0)
    for s in range(1, size):
        got = shift(total, axis, s, size)
        out = lax.dynamic_update_index_in_dim(out, got, lax.rem(me - s + size, size), 0)
    return out.reshape(value.shape)


def swap(blocks, sign, experts):
    moved = [
        lax.ppermute(block, "expert", [(i, (i + sign * (at + 1)) % experts) for i in range(experts)])
        for at, block in enumerate(blocks)
    ]
    return moved


def after(value, earlier):
    return lax.optimization_barrier((value, earlier))[0]


def body(
    sizes,
    tokens,
    segment_ids,
    offset_bucket,
    routes,
    capacity_keep,
    gain_attn,
    gain_ffn,
    w_query,
    w_key,
    w_value,
    w_output,
    rel_table,
    router,
    expert_in,
    expert_out,
    grad_out,
):
    length = segment_ids.shape[1]
    heads = rel_table.shape[1]
    inner = w_query.shape[1]
    head = inner // heads
    experts = router.shape[1]
    token_rows, width = tokens.shape
    capacity = token_rows * 5 // (4 * experts)
    slots = experts * capacity
    shard = w_query.shape[0]
    group_size = sizes["fsdp"] * sizes["expert"]
    own_buckets = rel_table.shape[0]
    buckets = own_buckets * group_size
    me = lax.axis_index("expert")
    ways, others = bits_of("fsdp", sizes["fsdp"]), bits_of("expert", sizes["expert"])
    keys = ways + others

    small_cols = [
        gain_attn[:, None],
        gain_ffn[:, None],
        router,
        jnp.pad(rel_table, ((0, shard - own_buckets), (0, 0))),
    ]
    used = 2 + experts + heads
    packed = jnp.concatenate(
        [w_query, w_key, w_value] + small_cols + [jnp.zeros((shard, -used % 128), BF)], axis=1
    )
    half = packed.shape[1] // 256 * 128
    gathered = jnp.concatenate(
        [
            gather_bits(packed[:, :half], others + ways, keys, sizes),
            gather_bits(packed[:, half:], ways[:-1] + others + ways[-1:], keys, sizes),
        ],
        axis=1,
    )
    proj_in = gathered[:, : 3 * inner]
    small = gathered[:, 3 * inner :]
    gain_one = small[:, 0].astype(F32)
    gain_two = small[:, 1].astype(F32)
    route_weight = small[:, 2 : 2 + experts]
    table = small[:, 2 + experts : used].reshape(group_size, shard, heads)[:, :own_buckets]
    table = table.reshape(buckets, heads)
    proj_output = lax.all_gather(after(w_output, gathered), GROUP, axis=0, tiled=True)

    chosen = routes[:, 0]
    picked = (chosen[:, None] == jnp.arange(experts, dtype=jnp.int32)[None, :]).astype(jnp.int32)
    earlier = jnp.cumsum(picked, axis=0) - picked
    slot = lax.rem(chosen - me + experts, experts) * capacity + jnp.sum(earlier * picked, axis=-1)
    slot = jnp.where(capacity_keep == 1, slot, slots)
    slot_ids = jnp.arange(slots, dtype=jnp.int32)
    to_slots = (slot_ids[:, None] == slot[None, :]).astype(BF)
    to_tokens = (slot[:, None] == slot_ids[None, :]).astype(BF)

    def leave(values, first, last):
        return dot32(to_slots[first:last], values).astype(BF)

    def depart(values):
        return [leave(values, s * capacity, (s + 1) * capacity) for s in range(1, experts)]

    g_local = leave(grad_out, 0, capacity)
    g_remote = jnp.concatenate(
        swap([after(block, gathered) for block in depart(grad_out)], 1, experts), axis=0
    )

    inputs = tokens.astype(F32)
    normed, scale_one = normalize(inputs, gain_one)
    normed_low = normed.astype(BF)
    qkv = dot32(normed_low, proj_in).astype(BF)

    bucket_of = jnp.concatenate([offset_bucket, jnp.full((1,), -1, jnp.int32)])
    hits = (bucket_of[None, :] == jnp.arange(buckets, dtype=jnp.int32)[:, None]).astype(BF)
    offsets = dot32(table.T, hits).reshape(heads // 2, 2, 2 * length)
    same = segment_ids[0][:, None] == jnp.arange(128, dtype=jnp.int32)[None, :]
    seg_q = jnp.where(same, 0.0, NEG).astype(BF)
    seg_k = same.astype(BF)
    attn_out, inverse, weights = attn_fwd(qkv, seg_q, seg_k, offsets, heads, head)

    resid = inputs + dot32(attn_out, proj_output)
    normed_two, scale_two = normalize(resid, gain_two)
    second_low = normed_two.astype(BF)

    x_remote = jnp.concatenate(swap(depart(second_low), 1, experts), axis=0)
    x_local = leave(second_low, 0, capacity)
    route_wide = jnp.pad(route_weight, ((0, 0), (0, 128 - experts)))
    mine = (jnp.arange(128, dtype=jnp.int32) == me).astype(F32)[None, :]
    shared = (route_wide, mine, expert_in, expert_out)
    act_l, du_l, deo_l = expert_hidden(x_local, g_local, *shared, experts)
    act_r, du_r, deo_r, d_in, d_out = expert_gradients(
        x_remote, g_remote, *shared, x_local, deo_l, act_l, du_l, experts
    )
    sum_in, sum_out = lax.psum((d_in, d_out), ("rep", "fsdp"))

    def cut(rows):
        return [rows[s * capacity : (s + 1) * capacity] for s in range(experts - 1)]

    geo_r, dn_r, dr_r = expert_results(
        x_remote, g_remote, *shared, after(act_r, d_in), du_r, experts
    )
    dn_back = swap(cut(dn_r), -1, experts)
    geo_l, dn_l, dr_l = expert_results(
        x_local, g_local, *shared, after(act_l, dn_r), du_l, experts
    )
    d_second = dot32(to_tokens, jnp.concatenate([dn_l] + dn_back, axis=0))
    geo_back = swap(cut(after(geo_r, dn_back[-1])), -1, experts)
    output = resid + dot32(to_tokens, jnp.concatenate([geo_l] + geo_back, axis=0))
    output = output.astype(BF)
    d_router = (dr_l + dr_r)[:experts].T

    cotangent = grad_out.astype(F32)
    d_resid_norm, d_gain_two = normalize_back(resid, scale_two, gain_two, d_second)
    d_resid = cotangent + d_resid_norm
    d_branch = d_resid.astype(BF)
    d_attn = dot_t(d_branch, proj_output).astype(BF)
    d_proj_output = lax.dot_general(
        attn_out, d_branch, (((0,), (0,)), ((), ())), preferred_element_type=F32
    ).astype(BF)
    d_query, d_key, d_value, d_offsets = attn_bwd(
        qkv, d_attn, attn_out, inverse, weights, 2 * length, heads, head
    )
    d_table = jnp.dot(
        hits.astype(F32), d_offsets.reshape(heads, 2 * length).T, precision=HIGH
    )
    d_qkv = jnp.concatenate([d_query, d_key, d_value], axis=1)
    d_proj = lax.dot_general(
        normed_low, d_qkv, (((0,), (0,)), ((), ())), preferred_element_type=F32
    ).astype(BF)
    d_normed = dot_t(d_qkv, proj_in)
    d_input_norm, d_gain_one = normalize_back(inputs, scale_one, gain_one, d_normed)
    grad_tokens = (d_resid + d_input_norm).astype(BF)

    d_small = jnp.concatenate(
        [
            d_gain_one[:, None],
            d_gain_two[:, None],
            d_router,
            jnp.pad(
                d_table.reshape(group_size, own_buckets, heads),
                ((0, 0), (0, shard - own_buckets), (0, 0)),
            ).reshape(width, heads),
            jnp.zeros((width, -used % 128), F32),
        ],
        axis=1,
    )
    order = ways[-1:] + others + ways[:-1]
    share_in, share_out, share_small = [
        sum_over(scatter_bits(value, order, keys, sizes), "rep", sizes["rep"])
        for value in (d_proj, d_proj_output, d_small)
    ]
    share_in = share_in.astype(F32)
    return (
        output,
        grad_tokens,
        share_small[:, 0],
        share_small[:, 1],
        share_in[:, :inner],
        share_in[:, inner : 2 * inner],
        share_in[:, 2 * inner :],
        share_out.astype(F32),
        share_small[:own_buckets, 2 + experts : used],
        share_small[:, 2 : 2 + experts],
        sum_in.astype(F32)[None],
        sum_out.astype(F32)[None],
    )


def solution(mesh):
    rows, group = P(("rep", "fsdp", "expert"), None), P(("fsdp", "expert"), None)
    flat_rows, flat_group = P(("rep", "fsdp", "expert")), P(("fsdp", "expert"))
    whole = P("expert", None, None)
    return jax.shard_map(
        functools.partial(body, dict(mesh.shape)),
        mesh=mesh,
        in_specs=(
            rows, rows, P(), rows, flat_rows, flat_group, flat_group,
            group, group, group, group, group, group, whole, whole, rows,
        ),
        out_specs=(
            rows, rows, flat_group, flat_group,
            group, group, group, group, group, group, whole, whole,
        ),
        check_vma=False,
    )
```

```python
import functools

import jax
import jax.numpy as jnp
from jax import lax
from jax.experimental import pallas as pl
from jax.experimental.pallas import tpu as pltpu
from jax.sharding import PartitionSpec as P

F32 = jnp.float32
BF = jnp.bfloat16
ROWS = 512
TILE = 128
VMEM_BYTES = 56 * 2**20


def dot_t(a, b):
    return lax.dot_general(a, b, (((1,), (1,)), ((), ())), preferred_element_type=F32)


def dot_n(a, b):
    return lax.dot_general(a, b, (((1,), (0,)), ((), ())), preferred_element_type=F32)


def skew(row, wide, out_ref):
    x = pltpu.roll(jnp.broadcast_to(row, (8, wide)), wide - (TILE - 1), 1)
    index = lax.broadcasted_iota(jnp.int32, x.shape, 0)
    for bit in (1, 2, 4):
        x = jnp.where((index & bit) != 0, pltpu.roll(x, bit, 1), x)
    n = 8
    while n < TILE:
        x = jnp.concatenate([x, pltpu.roll(x, n, 1)], axis=0)
        n *= 2
    out_ref[...] = x


def unskew(x, wide):
    n = x.shape[0]
    while n > 8:
        n //= 2
        x = x[:n] + pltpu.roll(x[n:], wide - n, 1)
    index = lax.broadcasted_iota(jnp.int32, x.shape, 0)
    for bit in (4, 2, 1):
        x = jnp.where((index & bit) != 0, pltpu.roll(x, wide - bit, 1), x)
    total = jnp.broadcast_to(jnp.sum(x, axis=0, keepdims=True), (8, wide))
    return pltpu.roll(total, TILE - 1, 1)[:1]


def attn_fwd_kernel(
    scaling, head, q_ref, k_ref, v_ref, sq_ref, sk_ref, off_ref, o_ref, inv_ref, e_ref, bias0, bias1
):
    length = q_ref.shape[0]
    wide = off_ref.shape[-1]
    lane = lax.broadcasted_iota(jnp.int32, (1, 2 * head), 1)
    firsts = lane < head
    bias = (bias0, bias1)
    for hh in range(2):
        skew(off_ref[0, hh : hh + 1, :], wide, bias[hh])
    kx = jnp.concatenate([k_ref[...], sk_ref[...]], axis=1)
    vx = v_ref[...]
    for b in range(length // ROWS):
        rows = pl.ds(b * ROWS, ROWS)
        q = q_ref[rows, :].astype(F32) * scaling
        made = []
        for hh in range(2):
            mine = firsts if hh == 0 else jnp.logical_not(firsts)
            qx = jnp.concatenate([jnp.where(mine, q, 0.0).astype(BF), sq_ref[rows, :]], axis=1)
            tiles = []
            for a in range(ROWS // TILE):
                at = length - TILE * (1 + a) - b * ROWS
                tiles.append(bias[hh][:, at : at + length])
            s = dot_t(qx, kx) + jnp.concatenate(tiles, axis=0)
            e = jnp.exp(s - jnp.max(s, axis=-1, keepdims=True)).astype(BF)
            e_ref[0, hh, rows, :] = e
            made.append(dot_n(e, jnp.where(mine, vx, jnp.ones_like(vx))))
        sums = jnp.where(firsts, pltpu.roll(made[0], head, 1), pltpu.roll(made[1], head, 1))
        inv = 1.0 / sums
        inv_ref[rows, :] = inv
        o_ref[rows, :] = (jnp.where(firsts, made[0], made[1]) * inv).astype(BF)


def attn_fwd(qkv, sq, sk, off, heads, head):
    length = qkv.shape[0]
    pairs = heads // 2
    wide = off.shape[-1]
    col = lambda at: pl.BlockSpec((length, 2 * head), lambda p: (0, at + p))
    fixed = pl.BlockSpec((length, 128), lambda p: (0, 0))
    return pl.pallas_call(
        functools.partial(attn_fwd_kernel, head**-0.5, head),
        grid=(pairs,),
        in_specs=[
            col(0), col(pairs), col(2 * pairs), fixed, fixed,
            pl.BlockSpec((1, 2, wide), lambda p: (p, 0, 0)),
        ],
        out_specs=[col(0), col(0), pl.BlockSpec((1, 2, length, length), lambda p: (p, 0, 0, 0))],
        out_shape=[
            jax.ShapeDtypeStruct((length, heads * head), BF),
            jax.ShapeDtypeStruct((length, heads * head), F32),
            jax.ShapeDtypeStruct((pairs, 2, length, length), BF),
        ],
        scratch_shapes=[pltpu.VMEM((TILE, wide), F32)] * 2,
        compiler_params=pltpu.CompilerParams(vmem_limit_bytes=VMEM_BYTES),
        cost_estimate=pl.CostEstimate(
            flops=40 * heads * length * length * head // 2,
            bytes_accessed=2 * heads * length * length,
            transcendentals=heads * length * length,
        ),
        name="attn_fwd",
    )(qkv, qkv, qkv, sq, sk, off)


def attn_bwd_kernel(
    scaling, head, q_ref, k_ref, v_ref, do_ref, o_ref, inv_ref, e_ref,
    dq_ref, dk_ref, dv_ref, doff_ref, acc0, acc1, dkt, dvt,
):
    length = q_ref.shape[0]
    wide = acc0.shape[-1]
    lane = lax.broadcasted_iota(jnp.int32, (1, 2 * head), 1)
    firsts = lane < head
    acc = (acc0, acc1)
    for ref in (acc0, acc1, dkt, dvt):
        ref[...] = jnp.zeros_like(ref)
    lane_b = lax.broadcasted_iota(jnp.int32, (ROWS, 128), 1)
    extra = jnp.where(lax.broadcasted_iota(jnp.int32, (length, 128), 1) < 2, 1.0, 0.0).astype(BF)
    vx = jnp.concatenate([v_ref[...], extra], axis=1)
    kx = k_ref[...]
    for b in range(length // ROWS):
        rows = pl.ds(b * ROWS, ROWS)
        do = do_ref[rows, :].astype(F32) * inv_ref[rows, :]
        toward = do * o_ref[rows, :].astype(F32)
        qt = q_ref[rows, :].T
        dot = do.astype(BF).T
        made = []
        for hh in range(2):
            mine = firsts if hh == 0 else jnp.logical_not(firsts)
            part = slice(hh * head, (hh + 1) * head)
            delta = -jnp.sum(jnp.where(mine, toward, 0.0), axis=-1, keepdims=True)
            hi = delta.astype(BF).astype(F32)
            ext = jnp.where(lane_b == 0, hi, jnp.where(lane_b == 1, delta - hi, 0.0)).astype(BF)
            dp = dot_t(jnp.concatenate([jnp.where(mine, do, 0.0).astype(BF), ext], axis=1), vx)
            e = e_ref[0, hh, rows, :]
            ds = e.astype(F32) * dp
            for a in range(ROWS // TILE):
                at = length - TILE * (1 + a) - b * ROWS
                acc[hh][:, at : at + length] += ds[a * TILE : (a + 1) * TILE]
            low = ds.astype(BF)
            made.append(dot_n(low, kx))
            dkt[part, :] += dot_n(qt[part], low)
            dvt[part, :] += dot_n(dot[part], e)
        dq_ref[rows, :] = (jnp.where(firsts, made[0], made[1]) * scaling).astype(BF)
    for hh in range(2):
        doff_ref[0, hh : hh + 1, :] = unskew(acc[hh][...], wide)
    dk_ref[...] = (dkt[...].T * scaling).astype(BF)
    dv_ref[...] = dvt[...].T.astype(BF)


def attn_bwd(qkv, do, o, inv, e, wide, heads, head):
    length = qkv.shape[0]
    pairs = heads // 2
    col = lambda at: pl.BlockSpec((length, 2 * head), lambda p: (0, at + p))
    return pl.pallas_call(
        functools.partial(attn_bwd_kernel, head**-0.5, head),
        grid=(pairs,),
        in_specs=[
            col(0), col(pairs), col(2 * pairs), col(0), col(0), col(0),
            pl.BlockSpec((1, 2, length, length), lambda p: (p, 0, 0, 0)),
        ],
        out_specs=[col(0), col(0), col(0), pl.BlockSpec((1, 2, wide), lambda p: (p, 0, 0))],
        out_shape=[jax.ShapeDtypeStruct((length, heads * head), BF)] * 3
        + [jax.ShapeDtypeStruct((pairs, 2, wide), F32)],
        scratch_shapes=[pltpu.VMEM((TILE, wide), F32)] * 2
        + [pltpu.VMEM((2 * head, length), F32)] * 2,
        compiler_params=pltpu.CompilerParams(vmem_limit_bytes=VMEM_BYTES),
        cost_estimate=pl.CostEstimate(
            flops=4 * heads * length * length * head // 2,
            bytes_accessed=heads * length * length // 4,
            transcendentals=0,
        ),
        name="attn_bwd",
    )(qkv, qkv, qkv, do, o, inv, e)
FF_BLOCK = 512


def gelu_pair(u):
    c = 0.7978845608028654
    sq = u * u
    t = jnp.tanh(u * (c + (0.044715 * c) * sq))
    half = 0.5 + 0.5 * t
    return u * half, half + (0.5 * u) * (1.0 - t * t) * (c + (3.0 * 0.044715 * c) * sq)


def probabilities(x, router, experts):
    logits = dot_n(x, router)
    lane = lax.broadcasted_iota(jnp.int32, logits.shape, 1)
    logits = jnp.where(lane < experts, logits, -1e30)
    e = jnp.exp(logits - jnp.max(logits, axis=-1, keepdims=True))
    return e / jnp.sum(e, axis=-1, keepdims=True)


def hidden_step(x_ref, deo_ref, win_ref, wout_ref, act_ref, du_ref):
    win, wout = win_ref[0], wout_ref[0]
    rows = x_ref.shape[0]
    parts = 2 if rows % 32 == 0 else 1
    step = rows // parts
    for at in range(0, rows, step):
        part = pl.ds(at, step)
        u = dot_n(x_ref[part, :], win)
        dact = dot_t(deo_ref[part, :], wout)
        a, slope = gelu_pair(u)
        act_ref[part, :] = a.astype(BF)
        du_ref[part, :] = (dact * slope).astype(BF)


def gated_cotangent(experts, x_ref, g_ref, router_ref, mine_ref, deo_ref):
    probs = probabilities(x_ref[...], router_ref[...], experts)
    gate = jnp.sum(probs * mine_ref[...], axis=-1, keepdims=True)
    deo_ref[...] = (gate * g_ref[...].astype(F32)).astype(BF)


def fixed(*shape):
    return pl.BlockSpec(shape, lambda f: (0,) * len(shape))


def in_block(width):
    return pl.BlockSpec((1, width, FF_BLOCK), lambda f: (0, 0, f))


def out_block(width):
    return pl.BlockSpec((1, FF_BLOCK, width), lambda f: (0, f, 0))


def slot_block(rows):
    return pl.BlockSpec((rows, FF_BLOCK), lambda f: (0, f))


def expert_kernel(
    experts, x_ref, g_ref, router_ref, mine_ref, win_ref, wout_ref,
    act_ref, du_ref, deo_ref, geo_ref, dn_ref, drouter_ref, eo, dx,
):
    @pl.when(pl.program_id(0) == 0)
    def _():
        gated_cotangent(experts, x_ref, g_ref, router_ref, mine_ref, deo_ref)
        eo[...] = jnp.zeros_like(eo)
        dx[...] = jnp.zeros_like(dx)

    hidden_step(x_ref, deo_ref, win_ref, wout_ref, act_ref, du_ref)
    eo[...] += dot_n(act_ref[...], wout_ref[0])
    dx[...] += dot_t(du_ref[...], win_ref[0])

    @pl.when(pl.program_id(0) == pl.num_programs(0) - 1)
    def _():
        finish(experts, x_ref, g_ref, router_ref, mine_ref, eo, dx, geo_ref, dn_ref, drouter_ref)


def expert(x, g, router, mine, win, wout, experts):
    rows, width = x.shape
    ff = win.shape[-1]
    return pl.pallas_call(
        functools.partial(expert_kernel, experts),
        grid=(ff // FF_BLOCK,),
        in_specs=[
            fixed(rows, width), fixed(rows, width), fixed(width, 128), fixed(1, 128),
            in_block(width), out_block(width),
        ],
        out_specs=[
            slot_block(rows), slot_block(rows), fixed(rows, width),
            fixed(rows, width), fixed(rows, width), fixed(128, width),
        ],
        out_shape=[
            jax.ShapeDtypeStruct((rows, ff), BF),
            jax.ShapeDtypeStruct((rows, ff), BF),
            jax.ShapeDtypeStruct((rows, width), BF),
            jax.ShapeDtypeStruct((rows, width), BF),
            jax.ShapeDtypeStruct((rows, width), BF),
            jax.ShapeDtypeStruct((128, width), F32),
        ],
        scratch_shapes=[pltpu.VMEM((rows, width), F32), pltpu.VMEM((rows, width), F32)],
        compiler_params=pltpu.CompilerParams(vmem_limit_bytes=VMEM_BYTES),
        cost_estimate=pl.CostEstimate(
            flops=16 * rows * width * ff,
            bytes_accessed=4 * width * ff + 4 * rows * ff,
            transcendentals=rows * ff,
        ),
        name="expert",
    )(x, g, router, mine, win, wout)


def weights_kernel(parts, *refs):
    xs, deos, acts, dus = (refs[i * parts : (i + 1) * parts] for i in range(4))
    din_ref, dout_ref = refs[4 * parts : 4 * parts + 2]
    turned = refs[4 * parts + 2 :]

    @pl.when(pl.program_id(0) == 0)
    def _():
        for t, x in zip(turned, xs):
            t[...] = x[...].T

    din = [dot_n(t[...], du[...]) for t, du in zip(turned, dus)]
    dout = [dot_n(act[...].T, deo[...]) for act, deo in zip(acts, deos)]
    din_ref[...] = sum(din[1:], din[0]).astype(BF)
    dout_ref[...] = sum(dout[1:], dout[0]).astype(BF)


def expert_weights(xs, deos, acts, dus):
    width = xs[0].shape[1]
    ff = acts[0].shape[1]
    parts = len(xs)
    total = sum(x.shape[0] for x in xs)
    return pl.pallas_call(
        functools.partial(weights_kernel, parts),
        grid=(ff // FF_BLOCK,),
        in_specs=[fixed(*x.shape) for x in xs]
        + [fixed(*deo.shape) for deo in deos]
        + [slot_block(act.shape[0]) for act in acts]
        + [slot_block(du.shape[0]) for du in dus],
        out_specs=[
            pl.BlockSpec((width, FF_BLOCK), lambda f: (0, f)),
            pl.BlockSpec((FF_BLOCK, width), lambda f: (f, 0)),
        ],
        out_shape=[
            jax.ShapeDtypeStruct((width, ff), BF),
            jax.ShapeDtypeStruct((ff, width), BF),
        ],
        scratch_shapes=[pltpu.VMEM((width, x.shape[0]), BF) for x in xs],
        compiler_params=pltpu.CompilerParams(vmem_limit_bytes=VMEM_BYTES),
        cost_estimate=pl.CostEstimate(
            flops=8 * total * width * ff,
            bytes_accessed=4 * width * ff + 4 * total * ff,
            transcendentals=0,
        ),
        name="expert_weights",
    )(*xs, *deos, *acts, *dus)


def finish(experts, x_ref, g_ref, router_ref, mine_ref, eo, dx, geo_ref, dn_ref, drouter_ref):
    made = eo[...].astype(BF).astype(F32)
    mine = mine_ref[...]
    probs = probabilities(x_ref[...], router_ref[...], experts)
    gate = jnp.sum(probs * mine, axis=-1, keepdims=True)
    geo_ref[...] = (gate * made).astype(BF)
    dgate = jnp.sum(made * g_ref[...].astype(F32), axis=-1, keepdims=True)
    dprobs = mine * dgate
    dlog = probs * (dprobs - jnp.sum(probs * dprobs, axis=-1, keepdims=True))
    dlog = dlog.astype(BF)
    dn_ref[...] = (dx[...] + dot_t(dlog, router_ref[...])).astype(BF)
    drouter_ref[...] = dot_n(dlog.T, x_ref[...])


EPS = 1e-06
NEG = -1e30
HIGH = lax.Precision.HIGHEST
GROUP = ("fsdp", "expert")


def normalize(values, gain):
    row_scale = lax.rsqrt(jnp.mean(values * values, axis=-1, keepdims=True) + EPS)
    return (values * row_scale * gain, row_scale)


def normalize_back(values, row_scale, gain, cotangent):
    weighted = cotangent * gain
    d_gain = jnp.sum(cotangent * values * row_scale, axis=0)
    d_values = row_scale * weighted - values * row_scale**3 * jnp.mean(
        weighted * values, axis=-1, keepdims=True
    )
    return (d_values, d_gain)


def dot32(left, right):
    return jnp.dot(left, right, preferred_element_type=F32)


def bits_of(axis, size):
    return [(axis, size >> (k + 1)) for k in range(size.bit_length() - 1)]


def partner(value, key, sizes):
    axis, bit = key
    return lax.ppermute(value, axis, [(i, i ^ bit) for i in range(sizes[axis])])


def side(key):
    return lax.rem(lax.axis_index(key[0]) // key[1], 2)


def gather_direct(value, keys, sizes):
    ways = sizes["expert"]
    near = keys.index(("fsdp", 1)) if ("fsdp", 1) in keys else None
    weights = [bit * (ways if axis == "fsdp" else 1) for axis, bit in keys]
    count = sizes["fsdp"] * ways
    far = [w for at, w in enumerate(weights) if at != near]
    masks = [0]
    for w in far:
        masks += [mask | w for mask in masks]
    me = lax.axis_index("fsdp") * ways + lax.axis_index("expert")
    blocks = []
    for mask in masks:
        got = value
        if mask:
            got = lax.ppermute(value, GROUP, [(i, i ^ mask) for i in range(count)])
        blocks.append((mask, got))
        if near is not None:
            mask_near = mask | weights[near]
            crossed = lax.ppermute(got, GROUP, [(i, i ^ weights[near]) for i in range(count)])
            blocks.append((mask_near, crossed))
    blocks = [block for _, block in sorted(blocks, key=lambda item: item[0])]
    for w in sorted(weights):
        swapped = lax.rem(me // w, 2) == 1
        blocks = [
            jnp.where(swapped, blocks[at ^ w], blocks[at]) for at in range(count)
        ]
    return jnp.concatenate(blocks, axis=0)


def scatter_bits(value, order, keys, sizes):
    held = list(keys)
    value = value.reshape((2,) * len(keys) + (value.shape[0] >> len(keys),) + value.shape[1:])
    for key in order:
        at = held.index(key)
        mine = side(key)
        got = partner(lax.dynamic_index_in_dim(value, 1 - mine, at, False), key, sizes)
        kept = lax.dynamic_index_in_dim(value, mine, at, False)
        value = (kept.astype(F32) + got.astype(F32)).astype(value.dtype)
        held.remove(key)
    return value


def shift(value, axis, by, size):
    return lax.ppermute(value, axis, [(i, (i + by) % size) for i in range(size)])


def sum_blocks(value, axis, size):
    me = lax.axis_index(axis)
    blocks = value.reshape((size, value.shape[0] // size) + value.shape[1:])
    total = lax.dynamic_index_in_dim(blocks, me, 0, False).astype(F32)
    for s in range(1, size):
        block = lax.dynamic_index_in_dim(blocks, lax.rem(me + s, size), 0, False)
        total = total + shift(block, axis, s, size).astype(F32)
    return total.astype(value.dtype)


def spread_blocks(total, axis, size):
    me = lax.axis_index(axis)
    out = jnp.zeros((size,) + total.shape, total.dtype)
    out = lax.dynamic_update_index_in_dim(out, total, me, 0)
    for s in range(1, size):
        got = shift(total, axis, s, size)
        out = lax.dynamic_update_index_in_dim(out, got, lax.rem(me - s + size, size), 0)
    return out.reshape((size * total.shape[0],) + total.shape[1:])


def sum_over(value, axis, size):
    return spread_blocks(sum_blocks(value, axis, size), axis, size)


def swap(blocks, sign, experts):
    moved = [
        lax.ppermute(block, "expert", [(i, (i + sign * (at + 1)) % experts) for i in range(experts)])
        for at, block in enumerate(blocks)
    ]
    return moved


def after(value, earlier):
    return lax.optimization_barrier((value, earlier))[0]


def body(
    sizes,
    tokens,
    segment_ids,
    offset_bucket,
    routes,
    capacity_keep,
    gain_attn,
    gain_ffn,
    w_query,
    w_key,
    w_value,
    w_output,
    rel_table,
    router,
    expert_in,
    expert_out,
    grad_out,
):
    length = segment_ids.shape[1]
    heads = rel_table.shape[1]
    inner = w_query.shape[1]
    head = inner // heads
    experts = router.shape[1]
    token_rows, width = tokens.shape
    capacity = token_rows * 5 // (4 * experts)
    slots = experts * capacity
    shard = w_query.shape[0]
    group_size = sizes["fsdp"] * sizes["expert"]
    own_buckets = rel_table.shape[0]
    buckets = own_buckets * group_size
    me = lax.axis_index("expert")
    ways, others = bits_of("fsdp", sizes["fsdp"]), bits_of("expert", sizes["expert"])
    keys = ways + others

    small_cols = [
        gain_attn[:, None],
        gain_ffn[:, None],
        router,
        jnp.pad(rel_table, ((0, shard - own_buckets), (0, 0))),
    ]
    used = 2 + experts + heads
    packed = jnp.concatenate(
        [w_query, w_key, w_value] + small_cols + [jnp.zeros((shard, -used % 128), BF)], axis=1
    )
    gathered = gather_direct(packed, keys, sizes)
    proj_in = gathered[:, : 3 * inner]
    small = gathered[:, 3 * inner :]
    gain_one = small[:, 0].astype(F32)
    gain_two = small[:, 1].astype(F32)
    route_weight = small[:, 2 : 2 + experts]
    table = small[:, 2 + experts : used].reshape(group_size, shard, heads)[:, :own_buckets]
    table = table.reshape(buckets, heads)
    proj_output = lax.all_gather(after(w_output, gathered), GROUP, axis=0, tiled=True)

    chosen = routes[:, 0]
    picked = (chosen[:, None] == jnp.arange(experts, dtype=jnp.int32)[None, :]).astype(jnp.int32)
    earlier = jnp.cumsum(picked, axis=0) - picked
    slot = lax.rem(chosen - me + experts, experts) * capacity + jnp.sum(earlier * picked, axis=-1)
    slot = jnp.where(capacity_keep == 1, slot, slots)
    slot_ids = jnp.arange(slots, dtype=jnp.int32)
    to_slots = (slot_ids[:, None] == slot[None, :]).astype(BF)
    to_tokens = (slot[:, None] == slot_ids[None, :]).astype(BF)

    def leave(values, first, last):
        return dot32(to_slots[first:last], values).astype(BF)

    def depart(values):
        return [leave(values, s * capacity, (s + 1) * capacity) for s in range(1, experts)]

    g_local = leave(grad_out, 0, capacity)
    g_remote = jnp.concatenate(
        swap([after(block, gathered) for block in depart(grad_out)], 1, experts), axis=0
    )

    inputs = tokens.astype(F32)
    normed, scale_one = normalize(inputs, gain_one)
    normed_low = normed.astype(BF)
    qkv = dot32(normed_low, proj_in).astype(BF)

    bucket_of = jnp.concatenate([offset_bucket, jnp.full((1,), -1, jnp.int32)])
    hits = (bucket_of[None, :] == jnp.arange(buckets, dtype=jnp.int32)[:, None]).astype(BF)
    offsets = dot32(table.T, hits).reshape(heads // 2, 2, 2 * length)
    same = segment_ids[0][:, None] == jnp.arange(128, dtype=jnp.int32)[None, :]
    seg_q = jnp.where(same, 0.0, NEG).astype(BF)
    seg_k = same.astype(BF)
    attn_out, inverse, weights = attn_fwd(qkv, seg_q, seg_k, offsets, heads, head)

    resid = inputs + dot32(attn_out, proj_output)
    normed_two, scale_two = normalize(resid, gain_two)
    second_low = normed_two.astype(BF)

    x_remote = jnp.concatenate(swap(depart(second_low), 1, experts), axis=0)
    x_local = leave(second_low, 0, capacity)
    route_wide = jnp.pad(route_weight, ((0, 0), (0, 128 - experts)))
    mine = (jnp.arange(128, dtype=jnp.int32) == me).astype(F32)[None, :]
    shared = (route_wide, mine, expert_in, expert_out)
    act_l, du_l, deo_l, geo_l, dn_l, dr_l = expert(x_local, g_local, *shared, experts)
    act_r, du_r, deo_r, geo_r, dn_r, dr_r = expert(x_remote, g_remote, *shared, experts)

    def cut(rows):
        return [rows[s * capacity : (s + 1) * capacity] for s in range(experts - 1)]

    dn_back = swap(cut(dn_r), -1, experts)
    d_in, d_out = expert_weights([x_local, x_remote], [deo_l, deo_r], [act_l, act_r], [du_l, du_r])
    sum_in, sum_out = lax.psum((d_in, d_out), ("rep", "fsdp"))
    d_second = dot32(to_tokens, jnp.concatenate([dn_l] + dn_back, axis=0))
    geo_back = swap(cut(after(geo_r, dn_back[-1])), -1, experts)
    output = resid + dot32(to_tokens, jnp.concatenate([geo_l] + geo_back, axis=0))
    output = output.astype(BF)
    d_router = (dr_l + dr_r)[:experts].T

    cotangent = grad_out.astype(F32)
    d_resid_norm, d_gain_two = normalize_back(resid, scale_two, gain_two, d_second)
    d_resid = cotangent + d_resid_norm
    d_branch = d_resid.astype(BF)
    d_attn = dot_t(d_branch, proj_output).astype(BF)
    d_proj_output = lax.dot_general(
        attn_out, d_branch, (((0,), (0,)), ((), ())), preferred_element_type=F32
    ).astype(BF)
    d_query, d_key, d_value, d_offsets = attn_bwd(
        qkv, d_attn, attn_out, inverse, weights, 2 * length, heads, head
    )
    d_table = jnp.dot(
        hits.astype(F32), d_offsets.reshape(heads, 2 * length).T, precision=HIGH
    )
    d_qkv = jnp.concatenate([d_query, d_key, d_value], axis=1)
    d_proj = lax.dot_general(
        normed_low, d_qkv, (((0,), (0,)), ((), ())), preferred_element_type=F32
    ).astype(BF)
    d_normed = dot_t(d_qkv, proj_in)
    d_input_norm, d_gain_one = normalize_back(inputs, scale_one, gain_one, d_normed)
    grad_tokens = (d_resid + d_input_norm).astype(BF)

    d_small = jnp.concatenate(
        [
            d_gain_one[:, None],
            d_gain_two[:, None],
            d_router,
            jnp.pad(
                d_table.reshape(group_size, own_buckets, heads),
                ((0, 0), (0, shard - own_buckets), (0, 0)),
            ).reshape(width, heads),
            jnp.zeros((width, -used % 128), F32),
        ],
        axis=1,
    )
    order = ways[-1:] + others + ways[:-1]
    share_in, share_out, share_small = [
        sum_over(scatter_bits(value, order, keys, sizes), "rep", sizes["rep"]).astype(F32)
        for value in (d_proj, d_proj_output, d_small)
    ]
    return (
        output,
        grad_tokens,
        share_small[:, 0],
        share_small[:, 1],
        share_in[:, :inner],
        share_in[:, inner : 2 * inner],
        share_in[:, 2 * inner :],
        share_out,
        share_small[:own_buckets, 2 + experts : used],
        share_small[:, 2 : 2 + experts],
        sum_in.astype(F32)[None],
        sum_out.astype(F32)[None],
    )


def solution(mesh):
    rows, group = P(("rep", "fsdp", "expert"), None), P(("fsdp", "expert"), None)
    flat_rows, flat_group = P(("rep", "fsdp", "expert")), P(("fsdp", "expert"))
    whole = P("expert", None, None)
    return jax.shard_map(
        functools.partial(body, dict(mesh.shape)),
        mesh=mesh,
        in_specs=(
            rows, rows, P(), rows, flat_rows, flat_group, flat_group,
            group, group, group, group, group, group, whole, whole, rows,
        ),
        out_specs=(
            rows, rows, flat_group, flat_group,
            group, group, group, group, group, group, whole, whole,
        ),
        check_vma=False,
    )
```

```python
import functools

import jax
import jax.numpy as jnp
from jax import lax
from jax.experimental import pallas as pl
from jax.experimental.pallas import tpu as pltpu
from jax.sharding import PartitionSpec as P

F32 = jnp.float32
BF = jnp.bfloat16
ROWS = 512
TILE = 128
VMEM_BYTES = 56 * 2**20


def dot_t(a, b):
    return lax.dot_general(a, b, (((1,), (1,)), ((), ())), preferred_element_type=F32)


def dot_n(a, b):
    return lax.dot_general(a, b, (((1,), (0,)), ((), ())), preferred_element_type=F32)


def skew(row, wide, out_ref):
    x = pltpu.roll(jnp.broadcast_to(row, (8, wide)), wide - (TILE - 1), 1)
    index = lax.broadcasted_iota(jnp.int32, x.shape, 0)
    for bit in (1, 2, 4):
        x = jnp.where((index & bit) != 0, pltpu.roll(x, bit, 1), x)
    n = 8
    while n < TILE:
        x = jnp.concatenate([x, pltpu.roll(x, n, 1)], axis=0)
        n *= 2
    out_ref[...] = x


def unskew(x, wide):
    n = x.shape[0]
    while n > 8:
        n //= 2
        x = x[:n] + pltpu.roll(x[n:], wide - n, 1)
    index = lax.broadcasted_iota(jnp.int32, x.shape, 0)
    for bit in (4, 2, 1):
        x = jnp.where((index & bit) != 0, pltpu.roll(x, wide - bit, 1), x)
    total = jnp.broadcast_to(jnp.sum(x, axis=0, keepdims=True), (8, wide))
    return pltpu.roll(total, TILE - 1, 1)[:1]


def attn_fwd_kernel(
    scaling, head, q_ref, k_ref, v_ref, sq_ref, sk_ref, off_ref, o_ref, inv_ref, e_ref, bias0, bias1
):
    length = q_ref.shape[0]
    wide = off_ref.shape[-1]
    lane = lax.broadcasted_iota(jnp.int32, (1, 2 * head), 1)
    firsts = lane < head
    bias = (bias0, bias1)
    for hh in range(2):
        skew(off_ref[0, hh : hh + 1, :], wide, bias[hh])
    kx = jnp.concatenate([k_ref[...], sk_ref[...]], axis=1)
    vx = v_ref[...]
    for b in range(length // ROWS):
        rows = pl.ds(b * ROWS, ROWS)
        q = q_ref[rows, :].astype(F32) * scaling
        made = []
        for hh in range(2):
            mine = firsts if hh == 0 else jnp.logical_not(firsts)
            qx = jnp.concatenate([jnp.where(mine, q, 0.0).astype(BF), sq_ref[rows, :]], axis=1)
            tiles = []
            for a in range(ROWS // TILE):
                at = length - TILE * (1 + a) - b * ROWS
                tiles.append(bias[hh][:, at : at + length])
            s = dot_t(qx, kx) + jnp.concatenate(tiles, axis=0)
            e = jnp.exp(s - jnp.max(s, axis=-1, keepdims=True)).astype(BF)
            e_ref[0, hh, rows, :] = e
            made.append(dot_n(e, jnp.where(mine, vx, jnp.ones_like(vx))))
        sums = jnp.where(firsts, pltpu.roll(made[0], head, 1), pltpu.roll(made[1], head, 1))
        inv = 1.0 / sums
        inv_ref[rows, :] = inv
        o_ref[rows, :] = (jnp.where(firsts, made[0], made[1]) * inv).astype(BF)


def attn_fwd(qkv, sq, sk, off, heads, head):
    length = qkv.shape[0]
    pairs = heads // 2
    wide = off.shape[-1]
    col = lambda at: pl.BlockSpec((length, 2 * head), lambda p: (0, at + p))
    fixed = pl.BlockSpec((length, 128), lambda p: (0, 0))
    return pl.pallas_call(
        functools.partial(attn_fwd_kernel, head**-0.5, head),
        grid=(pairs,),
        in_specs=[
            col(0), col(pairs), col(2 * pairs), fixed, fixed,
            pl.BlockSpec((1, 2, wide), lambda p: (p, 0, 0)),
        ],
        out_specs=[col(0), col(0), pl.BlockSpec((1, 2, length, length), lambda p: (p, 0, 0, 0))],
        out_shape=[
            jax.ShapeDtypeStruct((length, heads * head), BF),
            jax.ShapeDtypeStruct((length, heads * head), F32),
            jax.ShapeDtypeStruct((pairs, 2, length, length), BF),
        ],
        scratch_shapes=[pltpu.VMEM((TILE, wide), F32)] * 2,
        compiler_params=pltpu.CompilerParams(vmem_limit_bytes=VMEM_BYTES),
        cost_estimate=pl.CostEstimate(
            flops=40 * heads * length * length * head // 2,
            bytes_accessed=2 * heads * length * length,
            transcendentals=heads * length * length,
        ),
        name="attn_fwd",
    )(qkv, qkv, qkv, sq, sk, off)


def attn_bwd_kernel(
    scaling, head, q_ref, k_ref, v_ref, do_ref, o_ref, inv_ref, e_ref,
    dq_ref, dk_ref, dv_ref, doff_ref, acc0, acc1, dkt, dvt,
):
    length = q_ref.shape[0]
    wide = acc0.shape[-1]
    lane = lax.broadcasted_iota(jnp.int32, (1, 2 * head), 1)
    firsts = lane < head
    acc = (acc0, acc1)
    for ref in (acc0, acc1, dkt, dvt):
        ref[...] = jnp.zeros_like(ref)
    lane_b = lax.broadcasted_iota(jnp.int32, (ROWS, 128), 1)
    extra = jnp.where(lax.broadcasted_iota(jnp.int32, (length, 128), 1) < 2, 1.0, 0.0).astype(BF)
    vx = jnp.concatenate([v_ref[...], extra], axis=1)
    kx = k_ref[...]
    for b in range(length // ROWS):
        rows = pl.ds(b * ROWS, ROWS)
        do = do_ref[rows, :].astype(F32) * inv_ref[rows, :]
        toward = do * o_ref[rows, :].astype(F32)
        qt = q_ref[rows, :].T
        dot = do.astype(BF).T
        made = []
        for hh in range(2):
            mine = firsts if hh == 0 else jnp.logical_not(firsts)
            part = slice(hh * head, (hh + 1) * head)
            delta = -jnp.sum(jnp.where(mine, toward, 0.0), axis=-1, keepdims=True)
            hi = delta.astype(BF).astype(F32)
            ext = jnp.where(lane_b == 0, hi, jnp.where(lane_b == 1, delta - hi, 0.0)).astype(BF)
            dp = dot_t(jnp.concatenate([jnp.where(mine, do, 0.0).astype(BF), ext], axis=1), vx)
            e = e_ref[0, hh, rows, :]
            ds = e.astype(F32) * dp
            for a in range(ROWS // TILE):
                at = length - TILE * (1 + a) - b * ROWS
                acc[hh][:, at : at + length] += ds[a * TILE : (a + 1) * TILE]
            low = ds.astype(BF)
            made.append(dot_n(low, kx))
            dkt[part, :] += dot_n(qt[part], low)
            dvt[part, :] += dot_n(dot[part], e)
        dq_ref[rows, :] = (jnp.where(firsts, made[0], made[1]) * scaling).astype(BF)
    for hh in range(2):
        doff_ref[0, hh : hh + 1, :] = unskew(acc[hh][...], wide)
    dk_ref[...] = (dkt[...].T * scaling).astype(BF)
    dv_ref[...] = dvt[...].T.astype(BF)


def attn_bwd(qkv, do, o, inv, e, wide, heads, head):
    length = qkv.shape[0]
    pairs = heads // 2
    col = lambda at: pl.BlockSpec((length, 2 * head), lambda p: (0, at + p))
    return pl.pallas_call(
        functools.partial(attn_bwd_kernel, head**-0.5, head),
        grid=(pairs,),
        in_specs=[
            col(0), col(pairs), col(2 * pairs), col(0), col(0), col(0),
            pl.BlockSpec((1, 2, length, length), lambda p: (p, 0, 0, 0)),
        ],
        out_specs=[col(0), col(0), col(0), pl.BlockSpec((1, 2, wide), lambda p: (p, 0, 0))],
        out_shape=[jax.ShapeDtypeStruct((length, heads * head), BF)] * 3
        + [jax.ShapeDtypeStruct((pairs, 2, wide), F32)],
        scratch_shapes=[pltpu.VMEM((TILE, wide), F32)] * 2
        + [pltpu.VMEM((2 * head, length), F32)] * 2,
        compiler_params=pltpu.CompilerParams(vmem_limit_bytes=VMEM_BYTES),
        cost_estimate=pl.CostEstimate(
            flops=4 * heads * length * length * head // 2,
            bytes_accessed=heads * length * length // 4,
            transcendentals=0,
        ),
        name="attn_bwd",
    )(qkv, qkv, qkv, do, o, inv, e)
FF_BLOCK = 512


def gelu_pair(u):
    c = 0.7978845608028654
    sq = u * u
    t = jnp.tanh(u * (c + (0.044715 * c) * sq))
    half = 0.5 + 0.5 * t
    return u * half, half + (0.5 * u) * (1.0 - t * t) * (c + (3.0 * 0.044715 * c) * sq)


def probabilities(x, router, experts):
    logits = dot_n(x, router)
    lane = lax.broadcasted_iota(jnp.int32, logits.shape, 1)
    logits = jnp.where(lane < experts, logits, -1e30)
    e = jnp.exp(logits - jnp.max(logits, axis=-1, keepdims=True))
    return e / jnp.sum(e, axis=-1, keepdims=True)


def hidden_step(x_ref, deo_ref, win_ref, wout_ref, act_ref, du_ref):
    win, wout = win_ref[0], wout_ref[0]
    u = dot_n(x_ref[...], win)
    dact = dot_t(deo_ref[...], wout)
    a, slope = gelu_pair(u)
    act_ref[...] = a.astype(BF)
    du_ref[...] = (dact * slope).astype(BF)


def gated_cotangent(experts, x_ref, g_ref, router_ref, mine_ref, deo_ref):
    probs = probabilities(x_ref[...], router_ref[...], experts)
    gate = jnp.sum(probs * mine_ref[...], axis=-1, keepdims=True)
    deo_ref[...] = (gate * g_ref[...].astype(F32)).astype(BF)


def fixed(*shape):
    return pl.BlockSpec(shape, lambda f: (0,) * len(shape))


def in_block(width):
    return pl.BlockSpec((1, width, FF_BLOCK), lambda f: (0, 0, f))


def out_block(width):
    return pl.BlockSpec((1, FF_BLOCK, width), lambda f: (0, f, 0))


def slot_block(rows):
    return pl.BlockSpec((rows, FF_BLOCK), lambda f: (0, f))


def expert_kernel(
    experts, x_ref, g_ref, router_ref, mine_ref, win_ref, wout_ref,
    act_ref, du_ref, deo_ref, geo_ref, dn_ref, drouter_ref, eo, dx,
):
    @pl.when(pl.program_id(0) == 0)
    def _():
        gated_cotangent(experts, x_ref, g_ref, router_ref, mine_ref, deo_ref)
        eo[...] = jnp.zeros_like(eo)
        dx[...] = jnp.zeros_like(dx)

    hidden_step(x_ref, deo_ref, win_ref, wout_ref, act_ref, du_ref)
    eo[...] += dot_n(act_ref[...], wout_ref[0])
    dx[...] += dot_t(du_ref[...], win_ref[0])

    @pl.when(pl.program_id(0) == pl.num_programs(0) - 1)
    def _():
        finish(experts, x_ref, g_ref, router_ref, mine_ref, eo, dx, geo_ref, dn_ref, drouter_ref)


def expert(x, g, router, mine, win, wout, experts):
    rows, width = x.shape
    ff = win.shape[-1]
    return pl.pallas_call(
        functools.partial(expert_kernel, experts),
        grid=(ff // FF_BLOCK,),
        in_specs=[
            fixed(rows, width), fixed(rows, width), fixed(width, 128), fixed(1, 128),
            in_block(width), out_block(width),
        ],
        out_specs=[
            slot_block(rows), slot_block(rows), fixed(rows, width),
            fixed(rows, width), fixed(rows, width), fixed(128, width),
        ],
        out_shape=[
            jax.ShapeDtypeStruct((rows, ff), BF),
            jax.ShapeDtypeStruct((rows, ff), BF),
            jax.ShapeDtypeStruct((rows, width), BF),
            jax.ShapeDtypeStruct((rows, width), BF),
            jax.ShapeDtypeStruct((rows, width), BF),
            jax.ShapeDtypeStruct((128, width), F32),
        ],
        scratch_shapes=[pltpu.VMEM((rows, width), F32), pltpu.VMEM((rows, width), F32)],
        compiler_params=pltpu.CompilerParams(vmem_limit_bytes=VMEM_BYTES),
        cost_estimate=pl.CostEstimate(
            flops=16 * rows * width * ff,
            bytes_accessed=4 * width * ff + 4 * rows * ff,
            transcendentals=rows * ff,
        ),
        name="expert",
    )(x, g, router, mine, win, wout)


def weights_kernel(parts, *refs):
    xs, deos, acts, dus = (refs[i * parts : (i + 1) * parts] for i in range(4))
    din_ref, ahead_ref, rest_ref, turned = refs[4 * parts :]
    half = pl.num_programs(0) // 2

    def joined(values):
        return jnp.concatenate([value[...] for value in values], axis=0)

    @pl.when(pl.program_id(0) == 0)
    def _():
        turned[...] = joined(xs).T

    din_ref[...] = dot_n(turned[...], joined(dus)).astype(BF)
    dout = dot_n(joined(acts).T, joined(deos)).astype(BF)

    @pl.when(pl.program_id(0) < half)
    def _():
        ahead_ref[...] = dout

    @pl.when(pl.program_id(0) >= half)
    def _():
        rest_ref[...] = dout


def expert_weights(xs, deos, acts, dus):
    width = xs[0].shape[1]
    ff = acts[0].shape[1]
    parts = len(xs)
    total = sum(x.shape[0] for x in xs)
    half = ff // FF_BLOCK // 2
    return pl.pallas_call(
        functools.partial(weights_kernel, parts),
        grid=(ff // FF_BLOCK,),
        in_specs=[fixed(*x.shape) for x in xs]
        + [fixed(*deo.shape) for deo in deos]
        + [slot_block(act.shape[0]) for act in acts]
        + [slot_block(du.shape[0]) for du in dus],
        out_specs=[
            pl.BlockSpec((width, FF_BLOCK), lambda f: (0, f)),
            pl.BlockSpec((FF_BLOCK, width), lambda f: (jnp.minimum(f, half - 1), 0)),
            pl.BlockSpec((FF_BLOCK, width), lambda f: (jnp.maximum(f - half, 0), 0)),
        ],
        out_shape=[
            jax.ShapeDtypeStruct((width, ff), BF),
            jax.ShapeDtypeStruct((ff // 2, width), BF),
            jax.ShapeDtypeStruct((ff // 2, width), BF),
        ],
        scratch_shapes=[pltpu.VMEM((width, total), BF)],
        compiler_params=pltpu.CompilerParams(vmem_limit_bytes=VMEM_BYTES),
        cost_estimate=pl.CostEstimate(
            flops=8 * total * width * ff,
            bytes_accessed=4 * width * ff + 4 * total * ff,
            transcendentals=0,
        ),
        name="expert_weights",
    )(*xs, *deos, *acts, *dus)


def finish(experts, x_ref, g_ref, router_ref, mine_ref, eo, dx, geo_ref, dn_ref, drouter_ref):
    made = eo[...].astype(BF).astype(F32)
    mine = mine_ref[...]
    probs = probabilities(x_ref[...], router_ref[...], experts)
    gate = jnp.sum(probs * mine, axis=-1, keepdims=True)
    geo_ref[...] = (gate * made).astype(BF)
    dgate = jnp.sum(made * g_ref[...].astype(F32), axis=-1, keepdims=True)
    dprobs = mine * dgate
    dlog = probs * (dprobs - jnp.sum(probs * dprobs, axis=-1, keepdims=True))
    dlog = dlog.astype(BF)
    dn_ref[...] = (dx[...] + dot_t(dlog, router_ref[...])).astype(BF)
    drouter_ref[...] = dot_n(dlog.T, x_ref[...])


EPS = 1e-06
NEG = -1e30
HIGH = lax.Precision.HIGHEST
GROUP = ("fsdp", "expert")


def normalize(values, gain):
    row_scale = lax.rsqrt(jnp.mean(values * values, axis=-1, keepdims=True) + EPS)
    return (values * row_scale * gain, row_scale)


def normalize_back(values, row_scale, gain, cotangent):
    weighted = cotangent * gain
    d_gain = jnp.sum(cotangent * values * row_scale, axis=0)
    d_values = row_scale * weighted - values * row_scale**3 * jnp.mean(
        weighted * values, axis=-1, keepdims=True
    )
    return (d_values, d_gain)


def dot32(left, right):
    return jnp.dot(left, right, preferred_element_type=F32)


def bits_of(axis, size):
    return [(axis, size >> (k + 1)) for k in range(size.bit_length() - 1)]


def partner(value, key, sizes):
    axis, bit = key
    return lax.ppermute(value, axis, [(i, i ^ bit) for i in range(sizes[axis])])


def side(key):
    return lax.rem(lax.axis_index(key[0]) // key[1], 2)


def gather_direct(value, keys, sizes):
    ways = sizes["expert"]
    near = keys.index(("fsdp", 1)) if ("fsdp", 1) in keys else None
    weights = [bit * (ways if axis == "fsdp" else 1) for axis, bit in keys]
    count = sizes["fsdp"] * ways
    far = [w for at, w in enumerate(weights) if at != near]
    masks = [0]
    for w in far:
        masks += [mask | w for mask in masks]
    me = lax.axis_index("fsdp") * ways + lax.axis_index("expert")
    blocks = []
    for mask in masks:
        got = value
        if mask:
            got = lax.ppermute(value, GROUP, [(i, i ^ mask) for i in range(count)])
        blocks.append((mask, got))
        if near is not None:
            mask_near = mask | weights[near]
            crossed = lax.ppermute(got, GROUP, [(i, i ^ weights[near]) for i in range(count)])
            blocks.append((mask_near, crossed))
    blocks = [block for _, block in sorted(blocks, key=lambda item: item[0])]
    for w in sorted(weights):
        swapped = lax.rem(me // w, 2) == 1
        blocks = [
            jnp.where(swapped, blocks[at ^ w], blocks[at]) for at in range(count)
        ]
    return jnp.concatenate(blocks, axis=0)


def scatter_bits(value, order, keys, sizes):
    held = list(keys)
    value = value.reshape((2,) * len(keys) + (value.shape[0] >> len(keys),) + value.shape[1:])
    for key in order:
        at = held.index(key)
        mine = side(key)
        got = partner(lax.dynamic_index_in_dim(value, 1 - mine, at, False), key, sizes)
        kept = lax.dynamic_index_in_dim(value, mine, at, False)
        value = (kept.astype(F32) + got.astype(F32)).astype(value.dtype)
        held.remove(key)
    return value


def gather_ways(value, keys, sizes):
    for key in keys:
        got = partner(value, key, sizes)
        lower = side(key) == 0
        value = jnp.where(lower, jnp.stack([value, got]), jnp.stack([got, value]))
        value = value.reshape((-1,) + value.shape[2:])
    return value


def shift(value, axis, by, size):
    return lax.ppermute(value, axis, [(i, (i + by) % size) for i in range(size)])


def sum_blocks(value, axis, size):
    me = lax.axis_index(axis)
    blocks = value.reshape((size, value.shape[0] // size) + value.shape[1:])
    total = lax.dynamic_index_in_dim(blocks, me, 0, False).astype(F32)
    for s in range(1, size):
        block = lax.dynamic_index_in_dim(blocks, lax.rem(me + s, size), 0, False)
        total = total + shift(block, axis, s, size).astype(F32)
    return total.astype(value.dtype)


def spread_blocks(total, axis, size):
    me = lax.axis_index(axis)
    out = jnp.zeros((size,) + total.shape, total.dtype)
    out = lax.dynamic_update_index_in_dim(out, total, me, 0)
    for s in range(1, size):
        got = shift(total, axis, s, size)
        out = lax.dynamic_update_index_in_dim(out, got, lax.rem(me - s + size, size), 0)
    return out.reshape((size * total.shape[0],) + total.shape[1:])


def sum_over(value, axis, size):
    return spread_blocks(sum_blocks(value, axis, size), axis, size)


def swap(blocks, sign, experts):
    moved = [
        lax.ppermute(block, "expert", [(i, (i + sign * (at + 1)) % experts) for i in range(experts)])
        for at, block in enumerate(blocks)
    ]
    return moved


def after(value, earlier):
    return lax.optimization_barrier((value, earlier))[0]


def body(
    sizes,
    tokens,
    segment_ids,
    offset_bucket,
    routes,
    capacity_keep,
    gain_attn,
    gain_ffn,
    w_query,
    w_key,
    w_value,
    w_output,
    rel_table,
    router,
    expert_in,
    expert_out,
    grad_out,
):
    length = segment_ids.shape[1]
    heads = rel_table.shape[1]
    inner = w_query.shape[1]
    head = inner // heads
    experts = router.shape[1]
    token_rows, width = tokens.shape
    capacity = token_rows * 5 // (4 * experts)
    slots = experts * capacity
    shard = w_query.shape[0]
    group_size = sizes["fsdp"] * sizes["expert"]
    own_buckets = rel_table.shape[0]
    buckets = own_buckets * group_size
    me = lax.axis_index("expert")
    ways, others = bits_of("fsdp", sizes["fsdp"]), bits_of("expert", sizes["expert"])
    keys = ways + others

    small_cols = [
        gain_attn[:, None],
        gain_ffn[:, None],
        router,
        jnp.pad(rel_table, ((0, shard - own_buckets), (0, 0))),
    ]
    used = 2 + experts + heads
    packed = jnp.concatenate(
        [w_query, w_key, w_value] + small_cols + [jnp.zeros((shard, -used % 128), BF)], axis=1
    )
    gathered = gather_direct(packed, keys, sizes)
    proj_in = gathered[:, : 3 * inner]
    small = gathered[:, 3 * inner :]
    gain_one = small[:, 0].astype(F32)
    gain_two = small[:, 1].astype(F32)
    route_weight = small[:, 2 : 2 + experts]
    table = small[:, 2 + experts : used].reshape(group_size, shard, heads)[:, :own_buckets]
    table = table.reshape(buckets, heads)
    proj_output = lax.all_gather(after(w_output, gathered), GROUP, axis=0, tiled=True)

    chosen = routes[:, 0]
    picked = (chosen[:, None] == jnp.arange(experts, dtype=jnp.int32)[None, :]).astype(jnp.int32)
    earlier = jnp.cumsum(picked, axis=0) - picked
    slot = lax.rem(chosen - me + experts, experts) * capacity + jnp.sum(earlier * picked, axis=-1)
    slot = jnp.where(capacity_keep == 1, slot, slots)
    slot_ids = jnp.arange(slots, dtype=jnp.int32)
    to_slots = (slot_ids[:, None] == slot[None, :]).astype(BF)
    to_tokens = (slot[:, None] == slot_ids[None, :]).astype(BF)

    def leave(values, first, last):
        return dot32(to_slots[first:last], values).astype(BF)

    def depart(values):
        return [leave(values, s * capacity, (s + 1) * capacity) for s in range(1, experts)]

    g_local = leave(grad_out, 0, capacity)
    g_remote = jnp.concatenate(
        swap([after(block, gathered) for block in depart(grad_out)], 1, experts), axis=0
    )

    inputs = tokens.astype(F32)
    normed, scale_one = normalize(inputs, gain_one)
    normed_low = lax.optimization_barrier(normed.astype(BF))
    qkv = dot32(normed_low, proj_in).astype(BF)

    bucket_of = jnp.concatenate([offset_bucket, jnp.full((1,), -1, jnp.int32)])
    hits = (bucket_of[None, :] == jnp.arange(buckets, dtype=jnp.int32)[:, None]).astype(BF)
    offsets = dot32(table.T, hits).reshape(heads // 2, 2, 2 * length)
    same = segment_ids[0][:, None] == jnp.arange(128, dtype=jnp.int32)[None, :]
    seg_q = jnp.where(same, 0.0, NEG).astype(BF)
    seg_k = same.astype(BF)
    attn_out, inverse, weights = attn_fwd(qkv, seg_q, seg_k, offsets, heads, head)

    resid = inputs + dot32(attn_out, proj_output)
    normed_two, scale_two = normalize(resid, gain_two)
    second_low = normed_two.astype(BF)

    x_remote = jnp.concatenate(swap(depart(second_low), 1, experts), axis=0)
    x_local = leave(second_low, 0, capacity)
    route_wide = jnp.pad(route_weight, ((0, 0), (0, 128 - experts)))
    mine = (jnp.arange(128, dtype=jnp.int32) == me).astype(F32)[None, :]
    shared = (route_wide, mine, expert_in, expert_out)
    act_l, du_l, deo_l, geo_l, dn_l, dr_l = expert(x_local, g_local, *shared, experts)
    act_r, du_r, deo_r, geo_r, dn_r, dr_r = expert(x_remote, g_remote, *shared, experts)

    def cut(rows):
        return [rows[s * capacity : (s + 1) * capacity] for s in range(experts - 1)]

    dn_back = swap(cut(dn_r), -1, experts)
    d_in, d_ahead, d_rest = expert_weights([x_local, x_remote], [deo_l, deo_r], [act_l, act_r], [du_l, du_r])
    sum_in, sum_out = lax.psum((d_in, d_ahead), ("rep", "fsdp"))
    held = scatter_bits(d_rest, ways[-1:], ways[-1:], sizes)
    d_second = dot32(to_tokens, jnp.concatenate([dn_l] + dn_back, axis=0))
    geo_back = swap(cut(after(geo_r, dn_back[-1])), -1, experts)
    output = resid + dot32(to_tokens, jnp.concatenate([geo_l] + geo_back, axis=0))
    output = output.astype(BF)
    d_router = (dr_l + dr_r)[:experts].T

    cotangent = grad_out.astype(F32)
    d_resid_norm, d_gain_two = normalize_back(resid, scale_two, gain_two, d_second)
    d_resid = cotangent + d_resid_norm
    d_branch = d_resid.astype(BF)
    d_attn = dot_t(after(d_branch, held), proj_output).astype(BF)
    held = scatter_bits(held, ways[:-1][::-1], ways[:-1], sizes)
    d_proj_output = lax.dot_general(
        attn_out, d_branch, (((0,), (0,)), ((), ())), preferred_element_type=F32
    ).astype(BF)
    d_query, d_key, d_value, d_offsets = attn_bwd(
        qkv, d_attn, attn_out, inverse, weights, 2 * length, heads, head
    )
    d_table = jnp.dot(
        hits.astype(F32), d_offsets.reshape(heads, 2 * length).T, precision=HIGH
    )
    d_qkv = after(jnp.concatenate([d_query, d_key, d_value], axis=1), held)
    held = sum_blocks(held, "rep", sizes["rep"])
    d_proj = lax.dot_general(
        normed_low, d_qkv, (((0,), (0,)), ((), ())), preferred_element_type=F32
    ).astype(BF)
    packed = jnp.concatenate([d_proj, d_proj_output], axis=1)
    d_normed = dot_t(after(d_qkv, packed), proj_in)
    d_input_norm, d_gain_one = normalize_back(inputs, scale_one, gain_one, d_normed)
    grad_tokens = (d_resid + d_input_norm).astype(BF)

    d_small = jnp.concatenate(
        [
            d_gain_one[:, None],
            d_gain_two[:, None],
            d_router,
            jnp.pad(
                d_table.reshape(group_size, own_buckets, heads),
                ((0, 0), (0, shard - own_buckets), (0, 0)),
            ).reshape(width, heads),
            jnp.zeros((width, -used % 128), F32),
        ],
        axis=1,
    )
    order = ways[-1:] + others + ways[:-1]
    share, share_small = [
        sum_over(scatter_bits(value, order, keys, sizes), "rep", sizes["rep"]).astype(F32)
        for value in (packed, d_small)
    ]
    share_in, share_out = share[:, : 3 * inner], share[:, 3 * inner :]
    held = spread_blocks(held, "rep", sizes["rep"])
    sum_rest = gather_ways(held, ways, sizes)
    sum_out = jnp.concatenate([sum_out.astype(F32), sum_rest.astype(F32)], axis=0)
    return (
        output,
        grad_tokens,
        share_small[:, 0],
        share_small[:, 1],
        share_in[:, :inner],
        share_in[:, inner : 2 * inner],
        share_in[:, 2 * inner :],
        share_out,
        share_small[:own_buckets, 2 + experts : used],
        share_small[:, 2 : 2 + experts],
        sum_in.astype(F32)[None],
        sum_out[None],
    )


def solution(mesh):
    rows, group = P(("rep", "fsdp", "expert"), None), P(("fsdp", "expert"), None)
    flat_rows, flat_group = P(("rep", "fsdp", "expert")), P(("fsdp", "expert"))
    whole = P("expert", None, None)
    return jax.shard_map(
        functools.partial(body, dict(mesh.shape)),
        mesh=mesh,
        in_specs=(
            rows, rows, P(), rows, flat_rows, flat_group, flat_group,
            group, group, group, group, group, group, whole, whole, rows,
        ),
        out_specs=(
            rows, rows, flat_group, flat_group,
            group, group, group, group, group, group, whole, whole,
        ),
        check_vma=False,
    )
```

```python
import functools

import jax
import jax.numpy as jnp
from jax import lax
from jax.experimental import pallas as pl
from jax.experimental.pallas import tpu as pltpu
from jax.sharding import PartitionSpec as P

F32 = jnp.float32
BF = jnp.bfloat16
ROWS = 512
BACK_ROWS = 1024
TILE = 128
VMEM_BYTES = 56 * 2**20


def dot_t(a, b):
    return lax.dot_general(a, b, (((1,), (1,)), ((), ())), preferred_element_type=F32)


def dot_n(a, b):
    return lax.dot_general(a, b, (((1,), (0,)), ((), ())), preferred_element_type=F32)


def skew(row, wide, out_ref):
    x = pltpu.roll(jnp.broadcast_to(row, (8, wide)), wide - (TILE - 1), 1)
    index = lax.broadcasted_iota(jnp.int32, x.shape, 0)
    for bit in (1, 2, 4):
        x = jnp.where((index & bit) != 0, pltpu.roll(x, bit, 1), x)
    n = 8
    while n < TILE:
        x = jnp.concatenate([x, pltpu.roll(x, n, 1)], axis=0)
        n *= 2
    out_ref[...] = x


def unskew(x, wide):
    n = x.shape[0]
    while n > 8:
        n //= 2
        x = x[:n] + pltpu.roll(x[n:], wide - n, 1)
    index = lax.broadcasted_iota(jnp.int32, x.shape, 0)
    for bit in (4, 2, 1):
        x = jnp.where((index & bit) != 0, pltpu.roll(x, wide - bit, 1), x)
    total = jnp.broadcast_to(jnp.sum(x, axis=0, keepdims=True), (8, wide))
    return pltpu.roll(total, TILE - 1, 1)[:1]


def attn_fwd_kernel(
    scaling, head, q_ref, k_ref, v_ref, sq_ref, sk_ref, off_ref, o_ref, inv_ref, e_ref, bias0, bias1
):
    length = q_ref.shape[0]
    wide = off_ref.shape[-1]
    lane = lax.broadcasted_iota(jnp.int32, (1, 2 * head), 1)
    firsts = lane < head
    bias = (bias0, bias1)
    for hh in range(2):
        skew(off_ref[0, hh : hh + 1, :], wide, bias[hh])
    kx = jnp.concatenate([k_ref[...], sk_ref[...]], axis=1)
    vx = v_ref[...]
    for b in range(length // ROWS):
        rows = pl.ds(b * ROWS, ROWS)
        q = q_ref[rows, :].astype(F32) * scaling
        made = []
        for hh in range(2):
            mine = firsts if hh == 0 else jnp.logical_not(firsts)
            qx = jnp.concatenate([jnp.where(mine, q, 0.0).astype(BF), sq_ref[rows, :]], axis=1)
            tiles = []
            for a in range(ROWS // TILE):
                at = length - TILE * (1 + a) - b * ROWS
                tiles.append(bias[hh][:, at : at + length])
            s = dot_t(qx, kx) + jnp.concatenate(tiles, axis=0)
            e = jnp.exp(s - jnp.max(s, axis=-1, keepdims=True)).astype(BF)
            e_ref[0, hh, rows, :] = e
            made.append(dot_n(e, jnp.where(mine, vx, jnp.ones_like(vx))))
        sums = jnp.where(firsts, pltpu.roll(made[0], head, 1), pltpu.roll(made[1], head, 1))
        inv = 1.0 / sums
        inv_ref[rows, :] = inv
        o_ref[rows, :] = (jnp.where(firsts, made[0], made[1]) * inv).astype(BF)


def attn_fwd(qkv, sq, sk, off, heads, head):
    length = qkv.shape[0]
    pairs = heads // 2
    wide = off.shape[-1]
    col = lambda at: pl.BlockSpec((length, 2 * head), lambda p: (0, at + p))
    fixed = pl.BlockSpec((length, 128), lambda p: (0, 0))
    return pl.pallas_call(
        functools.partial(attn_fwd_kernel, head**-0.5, head),
        grid=(pairs,),
        in_specs=[
            col(0), col(pairs), col(2 * pairs), fixed, fixed,
            pl.BlockSpec((1, 2, wide), lambda p: (p, 0, 0)),
        ],
        out_specs=[col(0), col(0), pl.BlockSpec((1, 2, length, length), lambda p: (p, 0, 0, 0))],
        out_shape=[
            jax.ShapeDtypeStruct((length, heads * head), BF),
            jax.ShapeDtypeStruct((length, heads * head), F32),
            jax.ShapeDtypeStruct((pairs, 2, length, length), BF),
        ],
        scratch_shapes=[pltpu.VMEM((TILE, wide), F32)] * 2,
        compiler_params=pltpu.CompilerParams(vmem_limit_bytes=VMEM_BYTES),
        cost_estimate=pl.CostEstimate(
            flops=40 * heads * length * length * head // 2,
            bytes_accessed=2 * heads * length * length,
            transcendentals=heads * length * length,
        ),
        name="attn_fwd",
    )(qkv, qkv, qkv, sq, sk, off)


def attn_bwd_kernel(
    scaling, head, q_ref, k_ref, v_ref, do_ref, o_ref, inv_ref, e_ref,
    dq_ref, dk_ref, dv_ref, doff_ref, acc0, acc1, dkt, dvt,
):
    length = q_ref.shape[0]
    wide = acc0.shape[-1]
    lane = lax.broadcasted_iota(jnp.int32, (1, 2 * head), 1)
    firsts = lane < head
    acc = (acc0, acc1)
    for ref in (acc0, acc1, dkt, dvt):
        ref[...] = jnp.zeros_like(ref)
    lane_b = lax.broadcasted_iota(jnp.int32, (BACK_ROWS, 128), 1)
    extra = jnp.where(lax.broadcasted_iota(jnp.int32, (length, 128), 1) < 2, 1.0, 0.0).astype(BF)
    vx = jnp.concatenate([v_ref[...], extra], axis=1)
    kx = k_ref[...]
    for b in range(length // BACK_ROWS):
        rows = pl.ds(b * BACK_ROWS, BACK_ROWS)
        do = do_ref[rows, :].astype(F32) * inv_ref[rows, :]
        toward = do * o_ref[rows, :].astype(F32)
        qt = q_ref[rows, :].T
        dot = do.astype(BF).T
        made = []
        for hh in range(2):
            mine = firsts if hh == 0 else jnp.logical_not(firsts)
            part = slice(hh * head, (hh + 1) * head)
            delta = -jnp.sum(jnp.where(mine, toward, 0.0), axis=-1, keepdims=True)
            hi = delta.astype(BF).astype(F32)
            ext = jnp.where(lane_b == 0, hi, jnp.where(lane_b == 1, delta - hi, 0.0)).astype(BF)
            dp = dot_t(jnp.concatenate([jnp.where(mine, do, 0.0).astype(BF), ext], axis=1), vx)
            e = e_ref[0, hh, rows, :]
            ds = e.astype(F32) * dp
            for a in range(BACK_ROWS // TILE):
                at = length - TILE * (1 + a) - b * BACK_ROWS
                acc[hh][:, at : at + length] += ds[a * TILE : (a + 1) * TILE]
            low = ds.astype(BF)
            made.append(dot_n(low, kx))
            dkt[part, :] += dot_n(qt[part], low)
            dvt[part, :] += dot_n(dot[part], e)
        dq_ref[rows, :] = (jnp.where(firsts, made[0], made[1]) * scaling).astype(BF)
    for hh in range(2):
        doff_ref[0, hh : hh + 1, :] = unskew(acc[hh][...], wide)
    dk_ref[...] = (dkt[...].T * scaling).astype(BF)
    dv_ref[...] = dvt[...].T.astype(BF)


def attn_bwd(qkv, do, o, inv, e, wide, heads, head):
    length = qkv.shape[0]
    pairs = heads // 2
    col = lambda at: pl.BlockSpec((length, 2 * head), lambda p: (0, at + p))
    return pl.pallas_call(
        functools.partial(attn_bwd_kernel, head**-0.5, head),
        grid=(pairs,),
        in_specs=[
            col(0), col(pairs), col(2 * pairs), col(0), col(0), col(0),
            pl.BlockSpec((1, 2, length, length), lambda p: (p, 0, 0, 0)),
        ],
        out_specs=[col(0), col(0), col(0), pl.BlockSpec((1, 2, wide), lambda p: (p, 0, 0))],
        out_shape=[jax.ShapeDtypeStruct((length, heads * head), BF)] * 3
        + [jax.ShapeDtypeStruct((pairs, 2, wide), F32)],
        scratch_shapes=[pltpu.VMEM((TILE, wide), F32)] * 2
        + [pltpu.VMEM((2 * head, length), F32)] * 2,
        compiler_params=pltpu.CompilerParams(vmem_limit_bytes=VMEM_BYTES),
        cost_estimate=pl.CostEstimate(
            flops=4 * heads * length * length * head // 2,
            bytes_accessed=heads * length * length // 4,
            transcendentals=0,
        ),
        name="attn_bwd",
    )(qkv, qkv, qkv, do, o, inv, e)
FF_BLOCK = 512


def gelu_pair(u):
    c = 0.7978845608028654
    sq = u * u
    t = jnp.tanh(u * (c + (0.044715 * c) * sq))
    half = 0.5 + 0.5 * t
    return u * half, half + (0.5 * u) * (1.0 - t * t) * (c + (3.0 * 0.044715 * c) * sq)


def probabilities(x, router, experts):
    logits = dot_n(x, router)
    lane = lax.broadcasted_iota(jnp.int32, logits.shape, 1)
    logits = jnp.where(lane < experts, logits, -1e30)
    e = jnp.exp(logits - jnp.max(logits, axis=-1, keepdims=True))
    return e / jnp.sum(e, axis=-1, keepdims=True)


def hidden_step(x_ref, deo_ref, win_ref, wout_ref, act_ref, du_ref):
    win, wout = win_ref[0], wout_ref[0]
    u = dot_n(x_ref[...], win)
    dact = dot_t(deo_ref[...], wout)
    a, slope = gelu_pair(u)
    act_ref[...] = a.astype(BF)
    du_ref[...] = (dact * slope).astype(BF)


def gated_cotangent(experts, x_ref, g_ref, router_ref, mine_ref, deo_ref):
    probs = probabilities(x_ref[...], router_ref[...], experts)
    gate = jnp.sum(probs * mine_ref[...], axis=-1, keepdims=True)
    deo_ref[...] = (gate * g_ref[...].astype(F32)).astype(BF)


def fixed(*shape):
    return pl.BlockSpec(shape, lambda f: (0,) * len(shape))


def in_block(width):
    return pl.BlockSpec((1, width, FF_BLOCK), lambda f: (0, 0, f))


def out_block(width):
    return pl.BlockSpec((1, FF_BLOCK, width), lambda f: (0, f, 0))


def slot_block(rows):
    return pl.BlockSpec((rows, FF_BLOCK), lambda f: (0, f))


def expert_kernel(
    experts, x_ref, g_ref, router_ref, mine_ref, win_ref, wout_ref,
    act_ref, du_ref, deo_ref, geo_ref, dn_ref, drouter_ref, eo, dx,
):
    @pl.when(pl.program_id(0) == 0)
    def _():
        gated_cotangent(experts, x_ref, g_ref, router_ref, mine_ref, deo_ref)
        eo[...] = jnp.zeros_like(eo)
        dx[...] = jnp.zeros_like(dx)

    hidden_step(x_ref, deo_ref, win_ref, wout_ref, act_ref, du_ref)
    eo[...] += dot_n(act_ref[...], wout_ref[0])
    dx[...] += dot_t(du_ref[...], win_ref[0])

    @pl.when(pl.program_id(0) == pl.num_programs(0) - 1)
    def _():
        finish(experts, x_ref, g_ref, router_ref, mine_ref, eo, dx, geo_ref, dn_ref, drouter_ref)


def expert(x, g, router, mine, win, wout, experts):
    rows, width = x.shape
    ff = win.shape[-1]
    return pl.pallas_call(
        functools.partial(expert_kernel, experts),
        grid=(ff // FF_BLOCK,),
        in_specs=[
            fixed(rows, width), fixed(rows, width), fixed(width, 128), fixed(1, 128),
            in_block(width), out_block(width),
        ],
        out_specs=[
            slot_block(rows), slot_block(rows), fixed(rows, width),
            fixed(rows, width), fixed(rows, width), fixed(128, width),
        ],
        out_shape=[
            jax.ShapeDtypeStruct((rows, ff), BF),
            jax.ShapeDtypeStruct((rows, ff), BF),
            jax.ShapeDtypeStruct((rows, width), BF),
            jax.ShapeDtypeStruct((rows, width), BF),
            jax.ShapeDtypeStruct((rows, width), BF),
            jax.ShapeDtypeStruct((128, width), F32),
        ],
        scratch_shapes=[pltpu.VMEM((rows, width), F32), pltpu.VMEM((rows, width), F32)],
        compiler_params=pltpu.CompilerParams(vmem_limit_bytes=VMEM_BYTES),
        cost_estimate=pl.CostEstimate(
            flops=16 * rows * width * ff,
            bytes_accessed=4 * width * ff + 4 * rows * ff,
            transcendentals=rows * ff,
        ),
        name="expert",
    )(x, g, router, mine, win, wout)


def weights_kernel(parts, *refs):
    xs, deos, acts, dus = (refs[i * parts : (i + 1) * parts] for i in range(4))
    din_ref, ahead_ref, rest_ref, turned = refs[4 * parts :]
    half = pl.num_programs(0) // 2

    def joined(values):
        return jnp.concatenate([value[...] for value in values], axis=0)

    @pl.when(pl.program_id(0) == 0)
    def _():
        turned[...] = joined(xs).T

    din_ref[...] = dot_n(turned[...], joined(dus)).astype(BF)
    dout = dot_n(joined(acts).T, joined(deos)).astype(BF)

    @pl.when(pl.program_id(0) < half)
    def _():
        ahead_ref[...] = dout

    @pl.when(pl.program_id(0) >= half)
    def _():
        rest_ref[...] = dout


def expert_weights(xs, deos, acts, dus):
    width = xs[0].shape[1]
    ff = acts[0].shape[1]
    parts = len(xs)
    total = sum(x.shape[0] for x in xs)
    half = ff // FF_BLOCK // 2
    return pl.pallas_call(
        functools.partial(weights_kernel, parts),
        grid=(ff // FF_BLOCK,),
        in_specs=[fixed(*x.shape) for x in xs]
        + [fixed(*deo.shape) for deo in deos]
        + [slot_block(act.shape[0]) for act in acts]
        + [slot_block(du.shape[0]) for du in dus],
        out_specs=[
            pl.BlockSpec((width, FF_BLOCK), lambda f: (0, f)),
            pl.BlockSpec((FF_BLOCK, width), lambda f: (jnp.minimum(f, half - 1), 0)),
            pl.BlockSpec((FF_BLOCK, width), lambda f: (jnp.maximum(f - half, 0), 0)),
        ],
        out_shape=[
            jax.ShapeDtypeStruct((width, ff), BF),
            jax.ShapeDtypeStruct((ff // 2, width), BF),
            jax.ShapeDtypeStruct((ff // 2, width), BF),
        ],
        scratch_shapes=[pltpu.VMEM((width, total), BF)],
        compiler_params=pltpu.CompilerParams(vmem_limit_bytes=VMEM_BYTES),
        cost_estimate=pl.CostEstimate(
            flops=8 * total * width * ff,
            bytes_accessed=4 * width * ff + 4 * total * ff,
            transcendentals=0,
        ),
        name="expert_weights",
    )(*xs, *deos, *acts, *dus)


def finish(experts, x_ref, g_ref, router_ref, mine_ref, eo, dx, geo_ref, dn_ref, drouter_ref):
    made = eo[...].astype(BF).astype(F32)
    mine = mine_ref[...]
    probs = probabilities(x_ref[...], router_ref[...], experts)
    gate = jnp.sum(probs * mine, axis=-1, keepdims=True)
    geo_ref[...] = (gate * made).astype(BF)
    dgate = jnp.sum(made * g_ref[...].astype(F32), axis=-1, keepdims=True)
    dprobs = mine * dgate
    dlog = probs * (dprobs - jnp.sum(probs * dprobs, axis=-1, keepdims=True))
    dlog = dlog.astype(BF)
    dn_ref[...] = (dx[...] + dot_t(dlog, router_ref[...])).astype(BF)
    drouter_ref[...] = dot_n(dlog.T, x_ref[...])


EPS = 1e-06
NEG = -1e30
HIGH = lax.Precision.HIGHEST
GROUP = ("fsdp", "expert")


def normalize(values, gain):
    row_scale = lax.rsqrt(jnp.mean(values * values, axis=-1, keepdims=True) + EPS)
    return (values * row_scale * gain, row_scale)


def normalize_back(values, row_scale, gain, cotangent):
    weighted = cotangent * gain
    d_gain = jnp.sum(cotangent * values * row_scale, axis=0)
    d_values = row_scale * weighted - values * row_scale**3 * jnp.mean(
        weighted * values, axis=-1, keepdims=True
    )
    return (d_values, d_gain)


def dot32(left, right):
    return jnp.dot(left, right, preferred_element_type=F32)


def bits_of(axis, size):
    return [(axis, size >> (k + 1)) for k in range(size.bit_length() - 1)]


def partner(value, key, sizes):
    axis, bit = key
    return lax.ppermute(value, axis, [(i, i ^ bit) for i in range(sizes[axis])])


def side(key):
    return lax.rem(lax.axis_index(key[0]) // key[1], 2)


def gather_direct(value, keys, sizes):
    ways = sizes["expert"]
    near = keys.index(("fsdp", 1)) if ("fsdp", 1) in keys else None
    weights = [bit * (ways if axis == "fsdp" else 1) for axis, bit in keys]
    count = sizes["fsdp"] * ways
    far = [w for at, w in enumerate(weights) if at != near]
    masks = [0]
    for w in far:
        masks += [mask | w for mask in masks]
    me = lax.axis_index("fsdp") * ways + lax.axis_index("expert")
    blocks = []
    for mask in masks:
        got = value
        if mask:
            got = lax.ppermute(value, GROUP, [(i, i ^ mask) for i in range(count)])
        blocks.append((mask, got))
        if near is not None:
            mask_near = mask | weights[near]
            crossed = lax.ppermute(got, GROUP, [(i, i ^ weights[near]) for i in range(count)])
            blocks.append((mask_near, crossed))
    blocks = [block for _, block in sorted(blocks, key=lambda item: item[0])]
    for w in sorted(weights):
        swapped = lax.rem(me // w, 2) == 1
        blocks = [
            jnp.where(swapped, blocks[at ^ w], blocks[at]) for at in range(count)
        ]
    return jnp.concatenate(blocks, axis=0)


def scatter_bits(value, order, keys, sizes):
    held = list(keys)
    value = value.reshape((2,) * len(keys) + (value.shape[0] >> len(keys),) + value.shape[1:])
    for key in order:
        at = held.index(key)
        mine = side(key)
        got = partner(lax.dynamic_index_in_dim(value, 1 - mine, at, False), key, sizes)
        kept = lax.dynamic_index_in_dim(value, mine, at, False)
        value = (kept.astype(F32) + got.astype(F32)).astype(value.dtype)
        held.remove(key)
    return value


def gather_ways(value, keys, sizes):
    for key in keys:
        got = partner(value, key, sizes)
        lower = side(key) == 0
        value = jnp.where(lower, jnp.stack([value, got]), jnp.stack([got, value]))
        value = value.reshape((-1,) + value.shape[2:])
    return value


def shift(value, axis, by, size):
    return lax.ppermute(value, axis, [(i, (i + by) % size) for i in range(size)])


def sum_blocks(value, axis, size):
    me = lax.axis_index(axis)
    blocks = value.reshape((size, value.shape[0] // size) + value.shape[1:])
    total = lax.dynamic_index_in_dim(blocks, me, 0, False).astype(F32)
    for s in range(1, size):
        block = lax.dynamic_index_in_dim(blocks, lax.rem(me + s, size), 0, False)
        total = total + shift(block, axis, s, size).astype(F32)
    return total.astype(value.dtype)


def spread_blocks(total, axis, size):
    me = lax.axis_index(axis)
    out = jnp.zeros((size,) + total.shape, total.dtype)
    out = lax.dynamic_update_index_in_dim(out, total, me, 0)
    for s in range(1, size):
        got = shift(total, axis, s, size)
        out = lax.dynamic_update_index_in_dim(out, got, lax.rem(me - s + size, size), 0)
    return out.reshape((size * total.shape[0],) + total.shape[1:])


def sum_over(value, axis, size):
    return spread_blocks(sum_blocks(value, axis, size), axis, size)


def swap(blocks, sign, experts):
    moved = [
        lax.ppermute(block, "expert", [(i, (i + sign * (at + 1)) % experts) for i in range(experts)])
        for at, block in enumerate(blocks)
    ]
    return moved


def after(value, earlier):
    return lax.optimization_barrier((value, earlier))[0]


def body(
    sizes,
    tokens,
    segment_ids,
    offset_bucket,
    routes,
    capacity_keep,
    gain_attn,
    gain_ffn,
    w_query,
    w_key,
    w_value,
    w_output,
    rel_table,
    router,
    expert_in,
    expert_out,
    grad_out,
):
    length = segment_ids.shape[1]
    heads = rel_table.shape[1]
    inner = w_query.shape[1]
    head = inner // heads
    experts = router.shape[1]
    token_rows, width = tokens.shape
    capacity = token_rows * 5 // (4 * experts)
    slots = experts * capacity
    shard = w_query.shape[0]
    group_size = sizes["fsdp"] * sizes["expert"]
    own_buckets = rel_table.shape[0]
    buckets = own_buckets * group_size
    me = lax.axis_index("expert")
    ways, others = bits_of("fsdp", sizes["fsdp"]), bits_of("expert", sizes["expert"])
    keys = ways + others

    small_cols = [
        gain_attn[:, None],
        gain_ffn[:, None],
        router,
        jnp.pad(rel_table, ((0, shard - own_buckets), (0, 0))),
    ]
    used = 2 + experts + heads
    packed = jnp.concatenate(
        [w_query, w_key, w_value] + small_cols + [jnp.zeros((shard, -used % 128), BF)], axis=1
    )
    gathered = gather_direct(packed, keys, sizes)
    proj_in = gathered[:, : 3 * inner]
    small = gathered[:, 3 * inner :]
    gain_one = small[:, 0].astype(F32)
    gain_two = small[:, 1].astype(F32)
    route_weight = small[:, 2 : 2 + experts]
    table = small[:, 2 + experts : used].reshape(group_size, shard, heads)[:, :own_buckets]
    table = table.reshape(buckets, heads)
    proj_output = lax.all_gather(after(w_output, gathered), GROUP, axis=0, tiled=True)

    chosen = routes[:, 0]
    picked = (chosen[:, None] == jnp.arange(experts, dtype=jnp.int32)[None, :]).astype(jnp.int32)
    earlier = jnp.cumsum(picked, axis=0) - picked
    slot = lax.rem(chosen - me + experts, experts) * capacity + jnp.sum(earlier * picked, axis=-1)
    slot = jnp.where(capacity_keep == 1, slot, slots)
    slot_ids = jnp.arange(slots, dtype=jnp.int32)
    to_slots = (slot_ids[:, None] == slot[None, :]).astype(BF)
    to_tokens = (slot[:, None] == slot_ids[None, :]).astype(BF)

    def leave(values, first, last):
        return dot32(to_slots[first:last], values).astype(BF)

    def depart(values):
        return [leave(values, s * capacity, (s + 1) * capacity) for s in range(1, experts)]

    g_local = leave(grad_out, 0, capacity)
    g_remote = jnp.concatenate(
        swap([after(block, gathered) for block in depart(grad_out)], 1, experts), axis=0
    )

    inputs = tokens.astype(F32)
    normed, scale_one = normalize(inputs, gain_one)
    normed_low = lax.optimization_barrier(normed.astype(BF))
    qkv = dot32(normed_low, proj_in).astype(BF)

    bucket_of = jnp.concatenate([offset_bucket, jnp.full((1,), -1, jnp.int32)])
    hits = (bucket_of[None, :] == jnp.arange(buckets, dtype=jnp.int32)[:, None]).astype(BF)
    offsets = dot32(table.T, hits).reshape(heads // 2, 2, 2 * length)
    same = segment_ids[0][:, None] == jnp.arange(128, dtype=jnp.int32)[None, :]
    seg_q = jnp.where(same, 0.0, NEG).astype(BF)
    seg_k = same.astype(BF)
    attn_out, inverse, weights = attn_fwd(qkv, seg_q, seg_k, offsets, heads, head)

    resid = inputs + dot32(attn_out, proj_output)
    normed_two, scale_two = normalize(resid, gain_two)
    second_low = normed_two.astype(BF)

    x_remote = jnp.concatenate(swap(depart(second_low), 1, experts), axis=0)
    x_local = leave(second_low, 0, capacity)
    route_wide = jnp.pad(route_weight, ((0, 0), (0, 128 - experts)))
    mine = (jnp.arange(128, dtype=jnp.int32) == me).astype(F32)[None, :]
    shared = (route_wide, mine, expert_in, expert_out)
    act_l, du_l, deo_l, geo_l, dn_l, dr_l = expert(x_local, g_local, *shared, experts)
    act_r, du_r, deo_r, geo_r, dn_r, dr_r = expert(x_remote, g_remote, *shared, experts)

    def cut(rows):
        return [rows[s * capacity : (s + 1) * capacity] for s in range(experts - 1)]

    dn_back = swap(cut(dn_r), -1, experts)
    d_in, d_ahead, d_rest = expert_weights([x_local, x_remote], [deo_l, deo_r], [act_l, act_r], [du_l, du_r])
    sum_in, sum_out = lax.psum((d_in, d_ahead), ("rep", "fsdp"))
    held = scatter_bits(d_rest, ways[-1:], ways[-1:], sizes)
    d_second = dot32(to_tokens, jnp.concatenate([dn_l] + dn_back, axis=0))
    geo_back = swap(cut(after(geo_r, dn_back[-1])), -1, experts)
    output = resid + dot32(to_tokens, jnp.concatenate([geo_l] + geo_back, axis=0))
    output = output.astype(BF)
    d_router = (dr_l + dr_r)[:experts].T

    cotangent = grad_out.astype(F32)
    d_resid_norm, d_gain_two = normalize_back(resid, scale_two, gain_two, d_second)
    d_resid = cotangent + d_resid_norm
    d_branch = d_resid.astype(BF)
    d_attn = dot_t(after(d_branch, held), proj_output).astype(BF)
    held = scatter_bits(held, ways[:-1][::-1], ways[:-1], sizes)
    d_proj_output = lax.dot_general(
        attn_out, d_branch, (((0,), (0,)), ((), ())), preferred_element_type=F32
    ).astype(BF)
    d_query, d_key, d_value, d_offsets = attn_bwd(
        qkv, d_attn, attn_out, inverse, weights, 2 * length, heads, head
    )
    d_table = jnp.dot(
        hits.astype(F32), d_offsets.reshape(heads, 2 * length).T, precision=HIGH
    )
    d_qkv = after(jnp.concatenate([d_query, d_key, d_value], axis=1), held)
    held = sum_blocks(held, "rep", sizes["rep"])
    d_proj = lax.dot_general(
        normed_low, d_qkv, (((0,), (0,)), ((), ())), preferred_element_type=F32
    ).astype(BF)
    packed = jnp.concatenate([d_proj, d_proj_output], axis=1)
    d_normed = dot_t(after(d_qkv, packed), proj_in)
    d_input_norm, d_gain_one = normalize_back(inputs, scale_one, gain_one, d_normed)
    grad_tokens = (d_resid + d_input_norm).astype(BF)

    d_small = jnp.concatenate(
        [
            d_gain_one[:, None],
            d_gain_two[:, None],
            d_router,
            jnp.pad(
                d_table.reshape(group_size, own_buckets, heads),
                ((0, 0), (0, shard - own_buckets), (0, 0)),
            ).reshape(width, heads),
            jnp.zeros((width, -used % 128), F32),
        ],
        axis=1,
    )
    order = ways[-1:] + others + ways[:-1]
    share, share_small = [
        sum_over(scatter_bits(value, order, keys, sizes), "rep", sizes["rep"]).astype(F32)
        for value in (packed, d_small)
    ]
    share_in, share_out = share[:, : 3 * inner], share[:, 3 * inner :]
    held = spread_blocks(held, "rep", sizes["rep"])
    sum_rest = gather_ways(held, ways, sizes)
    sum_out = jnp.concatenate([sum_out.astype(F32), sum_rest.astype(F32)], axis=0)
    return (
        output,
        grad_tokens,
        share_small[:, 0],
        share_small[:, 1],
        share_in[:, :inner],
        share_in[:, inner : 2 * inner],
        share_in[:, 2 * inner :],
        share_out,
        share_small[:own_buckets, 2 + experts : used],
        share_small[:, 2 : 2 + experts],
        sum_in.astype(F32)[None],
        sum_out[None],
    )


def solution(mesh):
    rows, group = P(("rep", "fsdp", "expert"), None), P(("fsdp", "expert"), None)
    flat_rows, flat_group = P(("rep", "fsdp", "expert")), P(("fsdp", "expert"))
    whole = P("expert", None, None)
    return jax.shard_map(
        functools.partial(body, dict(mesh.shape)),
        mesh=mesh,
        in_specs=(
            rows, rows, P(), rows, flat_rows, flat_group, flat_group,
            group, group, group, group, group, group, whole, whole, rows,
        ),
        out_specs=(
            rows, rows, flat_group, flat_group,
            group, group, group, group, group, group, whole, whole,
        ),
        check_vma=False,
    )
```
